32 devices in a mesh: wa: 8 (over z, x), gx: 4 (over y, core).
Axes of the slice: x: 2, y: 2, z: 4, core: 2. Of those that a mesh axis runs over, the one named last changes fastest.
Arguments:
- field_a: float32 [2, 4, 768, 3840], P(None, 'gx', 'wa'), may hold values from -6 to 6
- field_b: float32 [2, 4, 768, 3840], P(None, 'gx', 'wa'), may hold values from -6 to 6
- keep_mask: int32 [3840], replicated, may hold values 0 or 1
- block_inv: float32 [6, 128, 128], replicated
- lower_mult: float32 [5, 128, 128], replicated, may hold values from -0.15 to 0.15
Outputs:
- new_a: float32 [2, 4, 768, 3840], P(None, 'gx', 'wa')
- new_b: float32 [2, 4, 768, 3840], P(None, 'gx', 'wa')
The draws below stay inside these ranges and needn't reach their ends.
All inputs are finite; a program needn't handle non-finite values.
Results may differ from the reference program's by a relative error of at most 0.0001.
Values sent between devices are 32-bit elements; how exact they have to be, the bound alone decides.
A program may use at most 192 MiB of HBM per device.

```python
import math
import jax
import jax.numpy as jnp
from jax import lax

NKZ = 3840
NY = 768
BLK = 128
NZ = 5760
NB = 6
KXT = 4


def draw_block_inv(key, part):
    own_key = jax.random.fold_in(key, 11)
    diag_key, rest_key = jax.random.split(own_key)
    diagonal = jnp.exp(jax.random.uniform(diag_key, (NB, BLK), jnp.float32, -0.6931, 0.6931))
    offdiag = jax.random.normal(rest_key, (NB, BLK, BLK), jnp.float32) * 0.03
    return offdiag + diagonal[:, :, None] * jnp.eye(BLK, dtype=jnp.float32)[None]


def set_ends(values, stream_key, smallest, top_value):
    longest = values.shape.index(max(values.shape))
    spots = []
    for shift in (0, 1):
        where = [jax.random.randint(jax.random.fold_in(stream_key, axis), (), 0, length) for axis, length in enumerate(values.shape)]
        where[longest] = (where[longest] + shift) % values.shape[longest]
        spots.append(tuple(where))
    return values.at[spots[0]].set(smallest).at[spots[1]].set(top_value)


def level_of(key, dims, shards, smallest, top_value):
    factor_of, own = 1.0, jax.random.fold_in(key, 6)
    for dim, shards_of in shards:
        draws = jnp.exp(jax.random.uniform(jax.random.fold_in(own, dim), (shards_of,), jnp.float32, smallest / len(shards), top_value / len(shards)))
        factor_of = factor_of * jnp.repeat(draws, dims[dim] // shards_of).reshape([-1 if axis == dim else 1 for axis in range(len(dims))])
    return factor_of


def centred(key, extent, scale, limit, cuts=(), kind=jnp.bfloat16):
    loudness = level_of(key, extent, cuts, -0.22, 0.18) if cuts else 1.0
    array = jax.random.normal(key, extent, jnp.float32) * scale * loudness
    return jnp.minimum(jnp.maximum(array, -limit), limit).astype(kind)


def setup_inputs(seed: int = 0) -> dict:
    keys = jax.random.split(jax.random.key(seed), 6)
    return {
        "field_a": centred(keys[0], (2, KXT, NY, NKZ), 1.0, 6.0, ((1, 4), (2, 8)), jnp.float32),
        "field_b": centred(keys[1], (2, KXT, NY, NKZ), 1.0, 6.0, ((1, 4), (2, 8)), jnp.float32),
        "keep_mask": set_ends((jax.random.randint(keys[2], (NKZ,), 0, 8) < 7).astype(jnp.int32), jax.random.fold_in(keys[2], 1), 0, 1),
        "block_inv": draw_block_inv(jax.random.fold_in(keys[5], 71), 0),
        "lower_mult": centred(keys[4], (NB - 1, BLK, BLK), 0.025, 0.15, (), jnp.float32),
    }


NL_COEFF = 0.25

def to_grid(field):
    half = NKZ // 2
    spectra = lax.complex(field[0], field[1])
    padding = jnp.zeros(spectra.shape[:-1] + (NZ - NKZ,), spectra.dtype)
    padded = jnp.concatenate([spectra[..., :half], padding, spectra[..., half:]], axis=-1)
    values = jnp.fft.ifft(padded, axis=-1) * (NZ / math.sqrt(NKZ))
    return (jnp.real(values), jnp.imag(values))

def to_modes(real_part, imag_part):
    half = NKZ // 2
    values = jnp.fft.fft(lax.complex(real_part, imag_part), axis=-1) / math.sqrt(NZ)
    kept = jnp.concatenate([values[..., :half], values[..., NZ - half:]], axis=-1)
    return (jnp.real(kept), jnp.imag(kept))

def complex_product(left_re, left_im, right_re, right_im):
    return (left_re * right_re - left_im * right_im, left_re * right_im + left_im * right_re)

def front(slab_a, slab_b, keep):
    a_re, a_im = to_grid(slab_a)
    b_re, b_im = to_grid(slab_b)
    p_re = jnp.zeros_like(a_re)
    p_im = jnp.zeros_like(a_re)
    q_re = jnp.zeros_like(a_re)
    q_im = jnp.zeros_like(a_re)
    for offset in range(KXT):
        ra_re = jnp.roll(a_re, offset, axis=0)
        ra_im = jnp.roll(a_im, offset, axis=0)
        rb_re = jnp.roll(b_re, offset, axis=0)
        rb_im = jnp.roll(b_im, offset, axis=0)
        ab_re, ab_im = complex_product(a_re[offset], a_im[offset], rb_re, rb_im)
        aa_re, aa_im = complex_product(a_re[offset], a_im[offset], ra_re, ra_im)
        bb_re, bb_im = complex_product(b_re[offset], b_im[offset], rb_re, rb_im)
        p_re = p_re + ab_re
        p_im = p_im + ab_im
        q_re = q_re + aa_re - bb_re
        q_im = q_im + aa_im - bb_im
    hp_re, hp_im = to_modes(p_re, p_im)
    hq_re, hq_im = to_modes(q_re, q_im)
    rhs_a = slab_a + NL_COEFF * jnp.stack([hp_re, hp_im]) * keep
    rhs_b = slab_b + NL_COEFF * jnp.stack([hq_re, hq_im]) * keep
    return (rhs_a, rhs_b)

def solve_rows(rhs, block_inv, lower_mult):
    shape = rhs.shape
    nblocks = block_inv.shape[0]
    width = block_inv.shape[1]
    vectors = jnp.swapaxes(rhs, 2, 3).reshape(-1, nblocks, width)
    blocks = jnp.moveaxis(vectors, 1, 0)

    def forward(previous, inputs):
        current, multiplier = inputs
        result = current - jnp.einsum('mc,rc->mr', previous, multiplier, precision=lax.Precision.HIGHEST)
        return (result, result)
    _, later = lax.scan(forward, blocks[0], (blocks[1:], lower_mult))
    reduced = jnp.concatenate([blocks[:1], later], axis=0)
    last = jnp.einsum('mc,rc->mr', reduced[-1], block_inv[-1], precision=lax.Precision.HIGHEST)

    def backward(following, inputs):
        current, inverse, multiplier = inputs
        result = jnp.einsum('mc,rc->mr', current, inverse, precision=lax.Precision.HIGHEST)
        result = result - jnp.einsum('mc,cr->mr', following, multiplier, precision=lax.Precision.HIGHEST)
        return (result, result)
    _, earlier = lax.scan(backward, last, (reduced[:-1], block_inv[:-1], lower_mult), reverse=True)
    solved = jnp.concatenate([earlier, last[None]], axis=0)
    solved = jnp.moveaxis(solved, 0, 1).reshape(shape[0], shape[1], shape[3], shape[2])
    return jnp.swapaxes(solved, 2, 3)

def reference(field_a, field_b, keep_mask, block_inv, lower_mult):
    keep = keep_mask.astype(field_a.dtype)
    rows = math.gcd(NY, 128)
    count = NY // rows

    def split(field):
        return jnp.moveaxis(field.reshape(2, KXT, count, rows, NKZ), 2, 0)

    def merge_back(blocks):
        return jnp.moveaxis(blocks, 0, 2).reshape(2, KXT, NY, NKZ)

    def one_block(pair):
        return front(pair[0], pair[1], keep)
    rhs_a, rhs_b = lax.map(one_block, (split(field_a), split(field_b)))
    new_a = solve_rows(merge_back(rhs_a), block_inv, lower_mult)
    new_b = solve_rows(merge_back(rhs_b), block_inv, lower_mult)
    return (new_a, new_b)
```

```python
import functools
import math

import jax
import jax.numpy as jnp
import ml_dtypes
import numpy as np
from jax import lax
from jax.experimental import pallas as pl
from jax.experimental.pallas import tpu as pltpu
from jax.sharding import PartitionSpec as P

NL_COEFF = 0.25
LANES = 128
ROWS = 8
KXT = 4


def add(x, y):
    return (x[0] + y[0], x[1] + y[1])


def sub(x, y):
    return (x[0] - y[0], x[1] - y[1])


def scaled(x, factor):
    return (x[0] * factor, x[1] * factor)


def times_i(x, sign):
    return (-x[1], x[0]) if sign > 0 else (x[1], -x[0])


def times(x, re, im):
    return (x[0] * re - x[1] * im, x[0] * im + x[1] * re)


def dft3(x, sign):
    both, diff = add(x[1], x[2]), sub(x[1], x[2])
    mid = sub(x[0], scaled(both, 0.5))
    turn = times_i(scaled(diff, math.sqrt(0.75)), sign)
    return [add(x[0], both), add(mid, turn), sub(mid, turn)]


def dft4(x, sign):
    even, odd = add(x[0], x[2]), add(x[1], x[3])
    even_d, odd_d = sub(x[0], x[2]), times_i(sub(x[1], x[3]), sign)
    return [add(even, odd), add(even_d, odd_d), sub(even, odd), sub(even_d, odd_d)]


def dft5(x, sign):
    c1, c2 = math.cos(2 * math.pi / 5), math.cos(4 * math.pi / 5)
    s1, s2 = math.sin(2 * math.pi / 5), math.sin(4 * math.pi / 5)
    t1, t2 = add(x[1], x[4]), add(x[2], x[3])
    t3, t4 = sub(x[1], x[4]), sub(x[2], x[3])
    m1 = add(x[0], add(scaled(t1, c1), scaled(t2, c2)))
    m2 = add(x[0], add(scaled(t1, c2), scaled(t2, c1)))
    n1 = times_i(add(scaled(t3, s1), scaled(t4, s2)), sign)
    n2 = times_i(sub(scaled(t3, s2), scaled(t4, s1)), sign)
    return [add(x[0], add(t1, t2)), add(m1, n1), add(m2, n2), sub(m2, n2), sub(m1, n1)]


def dft9(x, sign):
    inner = [dft3([x[j], x[3 + j], x[6 + j]], sign) for j in range(3)]
    out = [None] * 9
    for d1 in range(3):
        terms = []
        for j in range(3):
            angle = sign * 2 * math.pi * j * d1 / 9
            term = inner[j][d1]
            terms.append(times(term, math.cos(angle), math.sin(angle)) if j * d1 else term)
        for d2, value in enumerate(dft3(terms, sign)):
            out[d1 + 3 * d2] = value
    return out


def dft45(load, store, mid_ref, sign, shape):
    zero = jnp.zeros(shape, jnp.float32)
    for beta in range(9):
        ins = [load((9 * alpha + 5 * beta) % 45) for alpha in range(5)]
        ins = [(zero, zero) if v is None else v for v in ins]
        for c, value in enumerate(dft5(ins, sign)):
            mid_ref[c, beta, 0], mid_ref[c, beta, 1] = value
    for c in range(5):
        outs = dft9([(mid_ref[c, b, 0], mid_ref[c, b, 1]) for b in range(9)], sign)
        for d in range(9):
            spot = next(b for b in range(45) if b % 5 == c and b % 9 == d)
            store(spot, outs[d])


def split_dot(x, w_hi, w_lo):
    hi = x.astype(jnp.bfloat16)
    lo = (x - hi.astype(jnp.float32)).astype(jnp.bfloat16)
    dot = functools.partial(jnp.dot, preferred_element_type=jnp.float32)
    return dot(hi, w_hi) + (dot(lo, w_hi) + dot(hi, w_lo))


def front_kernel(a_ref, b_ref, keep_ref, twist_ref, winv_ref, wfwd_ref, out_ref,
                 plane_ref, mid_ref, za_ref, zb_ref, hat_ref):
    half = 15
    tile = (ROWS, LANES)
    for f, ref in enumerate((a_ref, b_ref)):
        for t in range(30):
            cols = pl.ds(t * LANES, LANES)
            ins = [(ref[0, k, :, cols], ref[1, k, :, cols]) for k in range(KXT)]
            for x, value in enumerate(dft4(ins, 1)):
                plane_ref[x, f, t, 0], plane_ref[x, f, t, 1] = value

    def one_plane(x, carry):
        for f, z_ref in enumerate((za_ref, zb_ref)):
            def load(m1):
                if half <= m1 < 30:
                    return None
                t = m1 if m1 < half else m1 - half
                return (plane_ref[x, f, t, 0], plane_ref[x, f, t, 1])

            def store(b, value):
                re, im = times(value, twist_ref[0, b : b + 1, :], twist_ref[1, b : b + 1, :])
                z_ref[b * ROWS : (b + 1) * ROWS, :LANES] = re
                z_ref[b * ROWS : (b + 1) * ROWS, LANES:] = im

            dft45(load, store, mid_ref, 1, tile)
        grid_a = split_dot(za_ref[...], winv_ref[0], winv_ref[1])
        grid_b = split_dot(zb_ref[...], winv_ref[0], winv_ref[1])
        a = (grid_a[:, :LANES], grid_a[:, LANES:])
        b = (grid_b[:, :LANES], grid_b[:, LANES:])
        p = times(a, b[0], b[1])
        total, diff = add(a, b), sub(a, b)
        q = times(total, diff[0], diff[1])
        for z_ref, value in ((za_ref, p), (zb_ref, q)):
            z_ref[...] = split_dot(jnp.concatenate(value, axis=1), wfwd_ref[0], wfwd_ref[1])
        for f, z_ref in enumerate((za_ref, zb_ref)):
            def load(b):
                rows = slice(b * ROWS, (b + 1) * ROWS)
                value = (z_ref[rows, :LANES], z_ref[rows, LANES:])
                return times(value, twist_ref[0, b : b + 1, :], -twist_ref[1, b : b + 1, :])

            def store(m1, value):
                if half <= m1 < 30:
                    return
                t = m1 if m1 < half else m1 - half
                hat_ref[x, f, t, 0], hat_ref[x, f, t, 1] = value

            dft45(load, store, mid_ref, -1, tile)
        return carry

    lax.fori_loop(0, KXT, one_plane, 0)
    for f, ref in enumerate((a_ref, b_ref)):
        for t in range(30):
            cols = pl.ds(t * LANES, LANES)
            keep = keep_ref[:, cols]
            ins = [(hat_ref[x, f, t, 0], hat_ref[x, f, t, 1]) for x in range(KXT)]
            into = pl.ds(t % half * LANES, LANES)
            for k, value in enumerate(dft4(ins, -1)):
                for part in range(2):
                    out_ref[f, part, t // half, k, :, into] = (
                        ref[part, k, :, cols] + value[part] * keep
                    )


def front_tables(modes):
    length = 3 * modes // 2
    b, m2 = np.arange(length // LANES)[:, None], np.arange(LANES)[None, :]
    twist = 2 * np.pi * (b * m2 % length) / length
    lane = np.arange(LANES)
    w = 2 * np.pi * (lane[:, None] * lane[None, :] % LANES) / LANES
    c, s = np.cos(w), np.sin(w)
    inv = np.block([[c, s], [-s, c]]) / math.sqrt(modes)
    fwd = np.block([[c, -s], [s, c]]) * (NL_COEFF / KXT / math.sqrt(length))

    def halves(table):
        hi = table.astype(np.float32).astype(ml_dtypes.bfloat16)
        lo = (table - hi.astype(np.float64)).astype(np.float32).astype(ml_dtypes.bfloat16)
        return np.stack([hi, lo])

    return np.stack([np.cos(twist), np.sin(twist)]).astype(np.float32), halves(inv), halves(fwd)


def front(slab_a, slab_b, keep):
    _, kxt, rows, modes = slab_a.shape
    assert kxt == KXT and modes == 30 * LANES and rows % ROWS == 0
    twist, inv, fwd = front_tables(modes)
    points = 45
    field_spec = pl.BlockSpec((2, KXT, ROWS, modes), lambda i: (0, 0, i, 0))
    return pl.pallas_call(
        front_kernel,
        grid=(rows // ROWS,),
        out_shape=jax.ShapeDtypeStruct((2, 2, 2, KXT, rows, modes // 2), jnp.float32),
        in_specs=[
            field_spec,
            field_spec,
            pl.BlockSpec((1, modes), lambda i: (0, 0)),
            pl.BlockSpec(twist.shape, lambda i: (0, 0, 0)),
            pl.BlockSpec(inv.shape, lambda i: (0, 0, 0)),
            pl.BlockSpec(fwd.shape, lambda i: (0, 0, 0)),
        ],
        out_specs=pl.BlockSpec((2, 2, 2, KXT, ROWS, modes // 2), lambda i: (0, 0, 0, 0, i, 0)),
        scratch_shapes=[
            pltpu.VMEM((KXT, 2, 30, 2, ROWS, LANES), jnp.float32),
            pltpu.VMEM((5, 9, 2, ROWS, LANES), jnp.float32),
            pltpu.VMEM((points * ROWS, 2 * LANES), jnp.float32),
            pltpu.VMEM((points * ROWS, 2 * LANES), jnp.float32),
            pltpu.VMEM((KXT, 2, 30, 2, ROWS, LANES), jnp.float32),
        ],
        compiler_params=pltpu.CompilerParams(vmem_limit_bytes=40 * 1024 * 1024),
        cost_estimate=pl.CostEstimate(
            flops=rows * 32 * 5760 * 256 * 6, bytes_accessed=rows * 2**18, transcendentals=0
        ),
    )(slab_a, slab_b, keep, jnp.asarray(twist), jnp.asarray(inv), jnp.asarray(fwd))


def solve_matrix(block_inv, lower_mult):
    count, width = block_inv.shape[:2]
    dot = functools.partial(jnp.matmul, precision=lax.Precision.HIGHEST)
    eye = jnp.eye(count * width, dtype=jnp.float32).reshape(count, width, count * width)
    reduced = [eye[0]]
    for j in range(1, count):
        reduced.append(eye[j] - dot(lower_mult[j - 1], reduced[-1]))
    own = dot(block_inv, jnp.stack(reduced))
    solved = [own[-1]]
    for j in range(count - 2, -1, -1):
        solved.insert(0, own[j] - dot(lower_mult[j].T, solved[0]))
    return jnp.concatenate(solved, axis=0)


def body(wa, gx, field_a, field_b, keep_mask, block_inv, lower_mult):
    _, _, rows, modes = field_a.shape
    keep = keep_mask.astype(jnp.float32).reshape(1, modes)
    padded = -(-rows // (gx * ROWS)) * gx * ROWS
    share = padded // gx

    def spread(field):
        field = field.reshape(2, rows, modes)
        if padded != rows:
            field = jnp.pad(field, ((0, 0), (0, padded - rows), (0, 0)))
        field = field.reshape(2, gx, share, modes)
        return lax.all_to_all(field, "gx", split_axis=1, concat_axis=1, tiled=True)

    rhs = front(spread(field_a), spread(field_b), keep)
    chunks = wa // 4
    width = modes // chunks
    if chunks != 2:
        rhs = jnp.moveaxis(rhs, 2, 4).reshape(2, 2, KXT, share, chunks, width)
        rhs = jnp.moveaxis(rhs, 4, 2)
    rhs = rhs.reshape(wa * gx, share, width)
    rhs = lax.all_to_all(rhs, ("wa", "gx"), split_axis=0, concat_axis=0, tiled=True)
    rhs = rhs.reshape(wa, padded, width)[:, :rows].reshape(wa * rows, width)
    solved = jnp.matmul(
        solve_matrix(block_inv, lower_mult), rhs, precision=lax.Precision.HIGH
    ).reshape(wa, rows, width)
    solved = lax.all_to_all(solved, "wa", split_axis=0, concat_axis=0, tiled=True)
    solved = solved.reshape(2, 2, chunks, rows, width)
    solved = jnp.moveaxis(solved, 2, 3).reshape(2, 2, 1, rows, modes)
    return (solved[0], solved[1])


def solution(mesh):
    return jax.shard_map(
        functools.partial(body, mesh.shape["wa"], mesh.shape["gx"]),
        mesh=mesh,
        in_specs=(P(None, "gx", "wa", None), P(None, "gx", "wa", None), P(), P(), P()),
        out_specs=(P(None, "gx", "wa", None), P(None, "gx", "wa", None)),
        check_vma=False,
    )
```

```python
import functools
import math

import jax
import jax.numpy as jnp
import ml_dtypes
import numpy as np
from jax import lax
from jax.experimental import pallas as pl
from jax.experimental.pallas import tpu as pltpu
from jax.sharding import PartitionSpec as P

NL_COEFF = 0.25
LANES = 128
ROWS = 8
KXT = 4


def add(x, y):
    return (x[0] + y[0], x[1] + y[1])


def sub(x, y):
    return (x[0] - y[0], x[1] - y[1])


def scaled(x, factor):
    return (x[0] * factor, x[1] * factor)


def times_i(x, sign):
    return (-x[1], x[0]) if sign > 0 else (x[1], -x[0])


def times(x, re, im):
    return (x[0] * re - x[1] * im, x[0] * im + x[1] * re)


def dft3(x, sign):
    both, diff = add(x[1], x[2]), sub(x[1], x[2])
    mid = sub(x[0], scaled(both, 0.5))
    turn = times_i(scaled(diff, math.sqrt(0.75)), sign)
    return [add(x[0], both), add(mid, turn), sub(mid, turn)]


def dft4(x, sign):
    even, odd = add(x[0], x[2]), add(x[1], x[3])
    even_d, odd_d = sub(x[0], x[2]), times_i(sub(x[1], x[3]), sign)
    return [add(even, odd), add(even_d, odd_d), sub(even, odd), sub(even_d, odd_d)]


def dft5(x, sign):
    c1, c2 = math.cos(2 * math.pi / 5), math.cos(4 * math.pi / 5)
    s1, s2 = math.sin(2 * math.pi / 5), math.sin(4 * math.pi / 5)
    t1, t2 = add(x[1], x[4]), add(x[2], x[3])
    t3, t4 = sub(x[1], x[4]), sub(x[2], x[3])
    m1 = add(x[0], add(scaled(t1, c1), scaled(t2, c2)))
    m2 = add(x[0], add(scaled(t1, c2), scaled(t2, c1)))
    n1 = times_i(add(scaled(t3, s1), scaled(t4, s2)), sign)
    n2 = times_i(sub(scaled(t3, s2), scaled(t4, s1)), sign)
    return [add(x[0], add(t1, t2)), add(m1, n1), add(m2, n2), sub(m2, n2), sub(m1, n1)]


def dft9(x, sign):
    inner = [dft3([x[j], x[3 + j], x[6 + j]], sign) for j in range(3)]
    out = [None] * 9
    for d1 in range(3):
        terms = []
        for j in range(3):
            angle = sign * 2 * math.pi * j * d1 / 9
            term = inner[j][d1]
            terms.append(times(term, math.cos(angle), math.sin(angle)) if j * d1 else term)
        for d2, value in enumerate(dft3(terms, sign)):
            out[d1 + 3 * d2] = value
    return out


def dft45(load, store, mid_ref, sign, shape):
    zero = jnp.zeros(shape, jnp.float32)
    for beta in range(9):
        ins = [load((9 * alpha + 5 * beta) % 45) for alpha in range(5)]
        ins = [(zero, zero) if v is None else v for v in ins]
        for c, value in enumerate(dft5(ins, sign)):
            mid_ref[c, beta, 0], mid_ref[c, beta, 1] = value
    for c in range(5):
        outs = dft9([(mid_ref[c, b, 0], mid_ref[c, b, 1]) for b in range(9)], sign)
        for d in range(9):
            spot = next(b for b in range(45) if b % 5 == c and b % 9 == d)
            store(spot, outs[d])


def split_dot(x, w_hi, w_lo):
    hi = x.astype(jnp.bfloat16)
    lo = (x - hi.astype(jnp.float32)).astype(jnp.bfloat16)
    dot = functools.partial(jnp.dot, preferred_element_type=jnp.float32)
    return dot(hi, w_hi) + (dot(lo, w_hi) + dot(hi, w_lo))


def front_kernel(a_ref, b_ref, keep_ref, twist_ref, winv_ref, wfwd_ref, out_ref,
                 plane_ref, mid_ref, za_ref, zb_ref, hat_ref):
    half = 15
    tile = (ROWS, LANES)
    for f, ref in enumerate((a_ref, b_ref)):
        for t in range(30):
            cols = pl.ds(t * LANES, LANES)
            ins = [(ref[0, k, :, cols], ref[1, k, :, cols]) for k in range(KXT)]
            for x, value in enumerate(dft4(ins, 1)):
                plane_ref[x, f, t, 0], plane_ref[x, f, t, 1] = value

    def one_plane(x, carry):
        for f, z_ref in enumerate((za_ref, zb_ref)):
            def load(m1):
                if half <= m1 < 30:
                    return None
                t = m1 if m1 < half else m1 - half
                return (plane_ref[x, f, t, 0], plane_ref[x, f, t, 1])

            def store(b, value):
                re, im = times(value, twist_ref[0, b : b + 1, :], twist_ref[1, b : b + 1, :])
                z_ref[b * ROWS : (b + 1) * ROWS, :LANES] = re
                z_ref[b * ROWS : (b + 1) * ROWS, LANES:] = im

            dft45(load, store, mid_ref, 1, tile)
        grid_a = split_dot(za_ref[...], winv_ref[0], winv_ref[1])
        grid_b = split_dot(zb_ref[...], winv_ref[0], winv_ref[1])
        a = (grid_a[:, :LANES], grid_a[:, LANES:])
        b = (grid_b[:, :LANES], grid_b[:, LANES:])
        p = times(a, b[0], b[1])
        total, diff = add(a, b), sub(a, b)
        q = times(total, diff[0], diff[1])
        for z_ref, value in ((za_ref, p), (zb_ref, q)):
            z_ref[...] = split_dot(jnp.concatenate(value, axis=1), wfwd_ref[0], wfwd_ref[1])
        for f, z_ref in enumerate((za_ref, zb_ref)):
            def load(b):
                rows = slice(b * ROWS, (b + 1) * ROWS)
                value = (z_ref[rows, :LANES], z_ref[rows, LANES:])
                return times(value, twist_ref[0, b : b + 1, :], -twist_ref[1, b : b + 1, :])

            def store(m1, value):
                if half <= m1 < 30:
                    return
                t = m1 if m1 < half else m1 - half
                hat_ref[x, f, t, 0], hat_ref[x, f, t, 1] = value

            dft45(load, store, mid_ref, -1, tile)
        return carry

    lax.fori_loop(0, KXT, one_plane, 0)
    for f, ref in enumerate((a_ref, b_ref)):
        for t in range(30):
            cols = pl.ds(t * LANES, LANES)
            keep = keep_ref[:, cols]
            ins = [(hat_ref[x, f, t, 0], hat_ref[x, f, t, 1]) for x in range(KXT)]
            for k, value in enumerate(dft4(ins, -1)):
                for part in range(2):
                    out_ref[f, part, k, :, cols] = ref[part, k, :, cols] + value[part] * keep


def front_tables(modes):
    length = 3 * modes // 2
    b, m2 = np.arange(length // LANES)[:, None], np.arange(LANES)[None, :]
    twist = 2 * np.pi * (b * m2 % length) / length
    lane = np.arange(LANES)
    w = 2 * np.pi * (lane[:, None] * lane[None, :] % LANES) / LANES
    c, s = np.cos(w), np.sin(w)
    inv = np.block([[c, s], [-s, c]]) / math.sqrt(modes)
    fwd = np.block([[c, -s], [s, c]]) * (NL_COEFF / KXT / math.sqrt(length))

    def halves(table):
        hi = table.astype(np.float32).astype(ml_dtypes.bfloat16)
        lo = (table - hi.astype(np.float64)).astype(np.float32).astype(ml_dtypes.bfloat16)
        return np.stack([hi, lo])

    return np.stack([np.cos(twist), np.sin(twist)]).astype(np.float32), halves(inv), halves(fwd)


def front(slab_a, slab_b, keep):
    _, kxt, rows, modes = slab_a.shape
    assert kxt == KXT and modes == 30 * LANES and rows % ROWS == 0
    twist, inv, fwd = front_tables(modes)
    points = 45
    field_spec = pl.BlockSpec((2, KXT, ROWS, modes), lambda i: (0, 0, i, 0))
    return pl.pallas_call(
        front_kernel,
        grid=(rows // ROWS,),
        out_shape=jax.ShapeDtypeStruct((2, 2, KXT, rows, modes), jnp.float32),
        in_specs=[
            field_spec,
            field_spec,
            pl.BlockSpec((1, modes), lambda i: (0, 0)),
            pl.BlockSpec(twist.shape, lambda i: (0, 0, 0)),
            pl.BlockSpec(inv.shape, lambda i: (0, 0, 0)),
            pl.BlockSpec(fwd.shape, lambda i: (0, 0, 0)),
        ],
        out_specs=pl.BlockSpec((2, 2, KXT, ROWS, modes), lambda i: (0, 0, 0, i, 0)),
        scratch_shapes=[
            pltpu.VMEM((KXT, 2, 30, 2, ROWS, LANES), jnp.float32),
            pltpu.VMEM((5, 9, 2, ROWS, LANES), jnp.float32),
            pltpu.VMEM((points * ROWS, 2 * LANES), jnp.float32),
            pltpu.VMEM((points * ROWS, 2 * LANES), jnp.float32),
            pltpu.VMEM((KXT, 2, 30, 2, ROWS, LANES), jnp.float32),
        ],
        compiler_params=pltpu.CompilerParams(vmem_limit_bytes=40 * 1024 * 1024),
        cost_estimate=pl.CostEstimate(
            flops=rows * 32 * 5760 * 256 * 6, bytes_accessed=rows * 2**18, transcendentals=0
        ),
    )(slab_a, slab_b, keep, jnp.asarray(twist), jnp.asarray(inv), jnp.asarray(fwd))


def solve_matrix(block_inv, lower_mult):
    count, width = block_inv.shape[:2]
    dot = functools.partial(jnp.matmul, precision=lax.Precision.HIGHEST)
    eye = jnp.eye(count * width, dtype=jnp.float32).reshape(count, width, count * width)
    reduced = [eye[0]]
    for j in range(1, count):
        reduced.append(eye[j] - dot(lower_mult[j - 1], reduced[-1]))
    own = dot(block_inv, jnp.stack(reduced))
    solved = [own[-1]]
    for j in range(count - 2, -1, -1):
        solved.insert(0, own[j] - dot(lower_mult[j].T, solved[0]))
    return jnp.concatenate(solved, axis=0)


def remote(src, dst, send_sem, recv_sem, wa, gx):
    return pltpu.make_async_remote_copy(
        src_ref=src, dst_ref=dst, send_sem=send_sem, recv_sem=recv_sem,
        device_id=(wa, gx), device_id_type=pl.DeviceIdType.MESH,
    )


def solve_kernel(chunks, group, gx_size, rhs_ref, up_ref, full_ref, out_ref,
                 held, solved, msg_out, msg_in,
                 send_sem, recv_sem, own_sem, msg_send, msg_recv, back_send, back_recv, back_own):
    wa, gx = lax.axis_index("wa"), lax.axis_index("gx")
    lane_count = rhs_ref.shape[-1] // chunks
    rows = out_ref.shape[1]
    base, spot = wa // group * group, wa % group
    partner = (wa + group) % (2 * group)
    count = group * gx_size
    me = spot * gx_size + gx
    barrier = pltpu.get_barrier_semaphore()
    for k in range(1, count):
        peer = (me + k) % count
        pl.semaphore_signal(barrier, inc=1, device_id=(base + peer // gx_size, peer % gx_size),
                            device_id_type=pl.DeviceIdType.MESH)
    pl.semaphore_signal(barrier, inc=1, device_id=(partner, gx),
                        device_id_type=pl.DeviceIdType.MESH)
    pl.semaphore_wait(barrier, count)

    def columns(c):
        return pl.ds(pl.multiple_of(c * lane_count, LANES), lane_count)

    def piece_to(c, k):
        peer = (me + k) % count
        return remote(rhs_ref.at[peer, :, columns(c)], held.at[me, :, columns(c)],
                      send_sem.at[c, k], recv_sem.at[c, k], base + peer // gx_size, peer % gx_size)

    def piece_from(c, k):
        peer = (me + count - k) % count
        return remote(rhs_ref.at[peer, :, columns(c)], held.at[peer, :, columns(c)],
                      send_sem.at[c, k], recv_sem.at[c, k], base + peer // gx_size, peer % gx_size)

    def own_piece(c):
        return pltpu.make_async_copy(rhs_ref.at[me, :, columns(c)], held.at[me, :, columns(c)],
                                     own_sem.at[c])

    def message(c):
        return remote(msg_out.at[:, columns(c)], msg_in.at[:, columns(c)],
                      msg_send.at[c], msg_recv.at[c], partner, gx)

    def back_to(c, k):
        peer = (spot + k) % group
        return remote(solved.at[peer, :, columns(c)], out_ref.at[spot, :, columns(c)],
                      back_send.at[c, k], back_recv.at[c, k], base + peer, gx)

    def back_from(c, k):
        peer = (spot + group - k) % group
        return remote(solved.at[peer, :, columns(c)], out_ref.at[peer, :, columns(c)],
                      back_send.at[c, k], back_recv.at[c, k], base + peer, gx)

    def back_own_piece(c):
        return pltpu.make_async_copy(solved.at[spot, :, columns(c)], out_ref.at[spot, :, columns(c)],
                                     back_own.at[c])

    def gathered(c):
        return held[:, :, columns(c)].reshape(group * rows, lane_count)

    def start_pieces(c, carry):
        own_piece(c).start()
        for k in range(1, count):
            piece_to(c, k).start()
        return carry

    def send_message(c, carry):
        own_piece(c).wait()
        for k in range(1, count):
            piece_from(c, k).wait_recv()
        msg_out[:, columns(c)] = split_matmul(up_ref[...], gathered(c))
        message(c).start()
        return carry

    def finish(c, carry):
        message(c).wait_recv()
        vectors = jnp.concatenate([gathered(c), msg_in[:, columns(c)]], axis=0)
        result = split_matmul(full_ref[...], vectors)
        solved[:, :, columns(c)] = result.reshape(group, rows, lane_count)
        back_own_piece(c).start()
        for k in range(1, group):
            back_to(c, k).start()
        return carry

    def drain(c, carry):
        for k in range(1, count):
            piece_to(c, k).wait_send()
        message(c).wait_send()
        back_own_piece(c).wait()
        for k in range(1, group):
            back_to(c, k).wait_send()
            back_from(c, k).wait_recv()
        return carry

    for step in (start_pieces, send_message, finish, drain):
        lax.fori_loop(0, chunks, step, 0)


def split_matmul(left, right):
    l_hi, r_hi = left.astype(jnp.bfloat16), right.astype(jnp.bfloat16)
    l_lo = (left - l_hi.astype(jnp.float32)).astype(jnp.bfloat16)
    r_lo = (right - r_hi.astype(jnp.float32)).astype(jnp.bfloat16)
    dot = functools.partial(jnp.dot, preferred_element_type=jnp.float32)
    return dot(l_hi, r_hi) + (dot(l_lo, r_hi) + dot(l_hi, r_lo))


def solve_across(wa, gx, rhs, block_inv, lower_mult):
    share, modes = rhs.shape[-2:]
    group = wa // 2
    count, width = group * gx, block_inv.shape[1]
    rows = share * gx
    half = group * rows
    middle = half // width
    dot = functools.partial(jnp.matmul, precision=lax.Precision.HIGHEST)
    dense = solve_matrix(block_inv, lower_mult)
    eye = jnp.eye(width, dtype=jnp.float32)
    state, answer = [eye], [-lower_mult[middle - 1].T]
    for j in range(middle - 2, -1, -1):
        state.insert(0, -dot(state[0], lower_mult[j]))
        answer.insert(0, -dot(lower_mult[j].T, answer[0]))
    low = lax.axis_index("wa") < group
    up = jnp.where(low, jnp.concatenate(state, axis=1), dense[half : half + width, half:])
    diagonal = jnp.where(low, dense[:half, :half], dense[half:, half:])
    side = jnp.where(low, jnp.concatenate(answer, axis=0), dense[half:, half - width : half])
    full = jnp.concatenate([diagonal, side], axis=1)
    chunks = 5
    dma = pltpu.SemaphoreType.DMA
    vmem = pl.BlockSpec(memory_space=pltpu.VMEM)
    anywhere = pl.BlockSpec(memory_space=pl.ANY)
    return pl.pallas_call(
        functools.partial(solve_kernel, chunks, group, gx),
        out_shape=jax.ShapeDtypeStruct((group, rows, modes), jnp.float32),
        in_specs=[anywhere, vmem, vmem],
        out_specs=anywhere,
        scratch_shapes=[
            pltpu.VMEM((count, share, modes), jnp.float32),
            pltpu.VMEM((group, rows, modes), jnp.float32),
            pltpu.VMEM((width, modes), jnp.float32),
            pltpu.VMEM((width, modes), jnp.float32),
            dma((chunks, count)),
            dma((chunks, count)),
            dma((chunks,)),
            dma((chunks,)),
            dma((chunks,)),
            dma((chunks, group)),
            dma((chunks, group)),
            dma((chunks,)),
        ],
        compiler_params=pltpu.CompilerParams(
            vmem_limit_bytes=40 * 1024 * 1024, collective_id=0, has_side_effects=True
        ),
    )(rhs.reshape(count, share, modes), up, full)


def body(wa, gx, field_a, field_b, keep_mask, block_inv, lower_mult):
    _, _, rows, modes = field_a.shape
    keep = keep_mask.astype(jnp.float32).reshape(1, modes)
    padded = -(-rows // (gx * ROWS)) * gx * ROWS
    share = padded // gx

    def spread(field):
        field = field.reshape(2, rows, modes)
        if padded != rows:
            field = jnp.pad(field, ((0, 0), (0, padded - rows), (0, 0)))
        field = field.reshape(2, gx, share, modes)
        return lax.all_to_all(field, "gx", split_axis=1, concat_axis=1, tiled=True)

    rhs = front(spread(field_a), spread(field_b), keep)
    if wa == 8 and gx == KXT and rows == padded and rows * 4 % block_inv.shape[1] == 0:
        solved = solve_across(wa, gx, rhs, block_inv, lower_mult)
        solved = solved.reshape(2, 2, 1, rows, modes)
        return (solved[0], solved[1])
    chunks = wa // 4
    width = modes // chunks
    rhs = jnp.moveaxis(rhs.reshape(2, 2, KXT, share, chunks, width), 4, 2)
    rhs = rhs.reshape(wa * gx, share, width)
    rhs = lax.all_to_all(rhs, ("wa", "gx"), split_axis=0, concat_axis=0, tiled=True)
    rhs = rhs.reshape(wa, padded, width)[:, :rows].reshape(wa * rows, width)
    solved = jnp.matmul(
        solve_matrix(block_inv, lower_mult), rhs, precision=lax.Precision.HIGH
    ).reshape(wa, rows, width)
    solved = lax.all_to_all(solved, "wa", split_axis=0, concat_axis=0, tiled=True)
    solved = solved.reshape(2, 2, chunks, rows, width)
    solved = jnp.moveaxis(solved, 2, 3).reshape(2, 2, 1, rows, modes)
    return (solved[0], solved[1])


def solution(mesh):
    return jax.shard_map(
        functools.partial(body, mesh.shape["wa"], mesh.shape["gx"]),
        mesh=mesh,
        in_specs=(P(None, "gx", "wa", None), P(None, "gx", "wa", None), P(), P(), P()),
        out_specs=(P(None, "gx", "wa", None), P(None, "gx", "wa", None)),
        check_vma=False,
    )
```

```python
import functools
import math

import jax
import jax.numpy as jnp
import ml_dtypes
import numpy as np
from jax import lax
from jax.experimental import pallas as pl
from jax.experimental.pallas import tpu as pltpu
from jax.sharding import PartitionSpec as P

NL_COEFF = 0.25
LANES = 128
ROWS = 8
KXT = 4


def add(x, y):
    return (x[0] + y[0], x[1] + y[1])


def sub(x, y):
    return (x[0] - y[0], x[1] - y[1])


def scaled(x, factor):
    return (x[0] * factor, x[1] * factor)


def times_i(x, sign):
    return (-x[1], x[0]) if sign > 0 else (x[1], -x[0])


def times(x, re, im):
    return (x[0] * re - x[1] * im, x[0] * im + x[1] * re)


def dft3(x, sign):
    both, diff = add(x[1], x[2]), sub(x[1], x[2])
    mid = sub(x[0], scaled(both, 0.5))
    turn = times_i(scaled(diff, math.sqrt(0.75)), sign)
    return [add(x[0], both), add(mid, turn), sub(mid, turn)]


def dft4(x, sign):
    even, odd = add(x[0], x[2]), add(x[1], x[3])
    even_d, odd_d = sub(x[0], x[2]), times_i(sub(x[1], x[3]), sign)
    return [add(even, odd), add(even_d, odd_d), sub(even, odd), sub(even_d, odd_d)]


def dft5(x, sign):
    c1, c2 = math.cos(2 * math.pi / 5), math.cos(4 * math.pi / 5)
    s1, s2 = math.sin(2 * math.pi / 5), math.sin(4 * math.pi / 5)
    t1, t2 = add(x[1], x[4]), add(x[2], x[3])
    t3, t4 = sub(x[1], x[4]), sub(x[2], x[3])
    m1 = add(x[0], add(scaled(t1, c1), scaled(t2, c2)))
    m2 = add(x[0], add(scaled(t1, c2), scaled(t2, c1)))
    n1 = times_i(add(scaled(t3, s1), scaled(t4, s2)), sign)
    n2 = times_i(sub(scaled(t3, s2), scaled(t4, s1)), sign)
    return [add(x[0], add(t1, t2)), add(m1, n1), add(m2, n2), sub(m2, n2), sub(m1, n1)]


def dft9(x, sign):
    inner = [dft3([x[j], x[3 + j], x[6 + j]], sign) for j in range(3)]
    out = [None] * 9
    for d1 in range(3):
        terms = []
        for j in range(3):
            angle = sign * 2 * math.pi * j * d1 / 9
            term = inner[j][d1]
            terms.append(times(term, math.cos(angle), math.sin(angle)) if j * d1 else term)
        for d2, value in enumerate(dft3(terms, sign)):
            out[d1 + 3 * d2] = value
    return out


def dft45(load, store, mid_ref, sign, shape):
    zero = jnp.zeros(shape, jnp.float32)
    for beta in range(9):
        ins = [load((9 * alpha + 5 * beta) % 45) for alpha in range(5)]
        ins = [(zero, zero) if v is None else v for v in ins]
        for c, value in enumerate(dft5(ins, sign)):
            mid_ref[c, beta, 0], mid_ref[c, beta, 1] = value
    for c in range(5):
        outs = dft9([(mid_ref[c, b, 0], mid_ref[c, b, 1]) for b in range(9)], sign)
        for d in range(9):
            spot = next(b for b in range(45) if b % 5 == c and b % 9 == d)
            store(spot, outs[d])


def split_dot(x, w_hi, w_lo):
    hi = x.astype(jnp.bfloat16)
    lo = (x - hi.astype(jnp.float32)).astype(jnp.bfloat16)
    dot = functools.partial(jnp.dot, preferred_element_type=jnp.float32)
    return dot(hi, w_hi) + (dot(lo, w_hi) + dot(hi, w_lo))


def front_kernel(a_ref, b_ref, keep_ref, twist_ref, winv_ref, wfwd_ref, out_ref,
                 plane_ref, mid_ref, za_ref, zb_ref, hat_ref):
    half = 15
    tile = (ROWS, LANES)
    for f, ref in enumerate((a_ref, b_ref)):
        for t in range(30):
            cols = pl.ds(t * LANES, LANES)
            ins = [(ref[0, k, :, cols], ref[1, k, :, cols]) for k in range(KXT)]
            for x, value in enumerate(dft4(ins, 1)):
                plane_ref[x, f, t, 0], plane_ref[x, f, t, 1] = value

    def one_plane(x, carry):
        for f, z_ref in enumerate((za_ref, zb_ref)):
            def load(m1):
                if half <= m1 < 30:
                    return None
                t = m1 if m1 < half else m1 - half
                return (plane_ref[x, f, t, 0], plane_ref[x, f, t, 1])

            def store(b, value):
                re, im = times(value, twist_ref[0, b : b + 1, :], twist_ref[1, b : b + 1, :])
                z_ref[b * ROWS : (b + 1) * ROWS, :LANES] = re
                z_ref[b * ROWS : (b + 1) * ROWS, LANES:] = im

            dft45(load, store, mid_ref, 1, tile)
        grid_a = split_dot(za_ref[...], winv_ref[0], winv_ref[1])
        grid_b = split_dot(zb_ref[...], winv_ref[0], winv_ref[1])
        a = (grid_a[:, :LANES], grid_a[:, LANES:])
        b = (grid_b[:, :LANES], grid_b[:, LANES:])
        p = times(a, b[0], b[1])
        total, diff = add(a, b), sub(a, b)
        q = times(total, diff[0], diff[1])
        for z_ref, value in ((za_ref, p), (zb_ref, q)):
            z_ref[...] = split_dot(jnp.concatenate(value, axis=1), wfwd_ref[0], wfwd_ref[1])
        for f, z_ref in enumerate((za_ref, zb_ref)):
            def load(b):
                rows = slice(b * ROWS, (b + 1) * ROWS)
                value = (z_ref[rows, :LANES], z_ref[rows, LANES:])
                return times(value, twist_ref[0, b : b + 1, :], -twist_ref[1, b : b + 1, :])

            def store(m1, value):
                if half <= m1 < 30:
                    return
                t = m1 if m1 < half else m1 - half
                hat_ref[x, f, t, 0], hat_ref[x, f, t, 1] = value

            dft45(load, store, mid_ref, -1, tile)
        return carry

    lax.fori_loop(0, KXT, one_plane, 0)
    for f, ref in enumerate((a_ref, b_ref)):
        for t in range(30):
            cols = pl.ds(t * LANES, LANES)
            keep = keep_ref[:, cols]
            ins = [(hat_ref[x, f, t, 0], hat_ref[x, f, t, 1]) for x in range(KXT)]
            for k, value in enumerate(dft4(ins, -1)):
                for part in range(2):
                    out_ref[f, part, k, :, cols] = ref[part, k, :, cols] + value[part] * keep


def front_tables(modes):
    length = 3 * modes // 2
    b, m2 = np.arange(length // LANES)[:, None], np.arange(LANES)[None, :]
    twist = 2 * np.pi * (b * m2 % length) / length
    lane = np.arange(LANES)
    w = 2 * np.pi * (lane[:, None] * lane[None, :] % LANES) / LANES
    c, s = np.cos(w), np.sin(w)
    inv = np.block([[c, s], [-s, c]]) / math.sqrt(modes)
    fwd = np.block([[c, -s], [s, c]]) * (NL_COEFF / KXT / math.sqrt(length))

    def halves(table):
        hi = table.astype(np.float32).astype(ml_dtypes.bfloat16)
        lo = (table - hi.astype(np.float64)).astype(np.float32).astype(ml_dtypes.bfloat16)
        return np.stack([hi, lo])

    return np.stack([np.cos(twist), np.sin(twist)]).astype(np.float32), halves(inv), halves(fwd)


def front(slab_a, slab_b, keep):
    _, kxt, rows, modes = slab_a.shape
    assert kxt == KXT and modes == 30 * LANES and rows % ROWS == 0
    twist, inv, fwd = front_tables(modes)
    points = 45
    field_spec = pl.BlockSpec((2, KXT, ROWS, modes), lambda i: (0, 0, i, 0))
    return pl.pallas_call(
        front_kernel,
        grid=(rows // ROWS,),
        out_shape=jax.ShapeDtypeStruct((2, 2, KXT, rows, modes), jnp.float32),
        in_specs=[
            field_spec,
            field_spec,
            pl.BlockSpec((1, modes), lambda i: (0, 0)),
            pl.BlockSpec(twist.shape, lambda i: (0, 0, 0)),
            pl.BlockSpec(inv.shape, lambda i: (0, 0, 0)),
            pl.BlockSpec(fwd.shape, lambda i: (0, 0, 0)),
        ],
        out_specs=pl.BlockSpec((2, 2, KXT, ROWS, modes), lambda i: (0, 0, 0, i, 0)),
        scratch_shapes=[
            pltpu.VMEM((KXT, 2, 30, 2, ROWS, LANES), jnp.float32),
            pltpu.VMEM((5, 9, 2, ROWS, LANES), jnp.float32),
            pltpu.VMEM((points * ROWS, 2 * LANES), jnp.float32),
            pltpu.VMEM((points * ROWS, 2 * LANES), jnp.float32),
            pltpu.VMEM((KXT, 2, 30, 2, ROWS, LANES), jnp.float32),
        ],
        compiler_params=pltpu.CompilerParams(vmem_limit_bytes=40 * 1024 * 1024),
        cost_estimate=pl.CostEstimate(
            flops=rows * 32 * 5760 * 256 * 6, bytes_accessed=rows * 2**18, transcendentals=0
        ),
    )(slab_a, slab_b, keep, jnp.asarray(twist), jnp.asarray(inv), jnp.asarray(fwd))


def solve_matrices(block_inv, lower_mult):
    count, width = block_inv.shape[:2]
    dot = functools.partial(jnp.matmul, precision=lax.Precision.HIGHEST)
    eye = jnp.eye(count * width, dtype=jnp.float32).reshape(count, width, count * width)
    reduced = [eye[0]]
    for j in range(1, count):
        reduced.append(eye[j] - dot(lower_mult[j - 1], reduced[-1]))
    back = [eye[-1]]
    for j in range(count - 2, -1, -1):
        back.insert(0, eye[j] - dot(lower_mult[j].T, back[0]))
    reduced = jnp.stack(reduced)
    back = jnp.concatenate(back, axis=0)
    dense = dot(back, dot(block_inv, reduced).reshape(count * width, count * width))
    return reduced.reshape(count * width, count * width), back, dense


def remote(src, dst, send_sem, recv_sem, wa, gx):
    return pltpu.make_async_remote_copy(
        src_ref=src, dst_ref=dst, send_sem=send_sem, recv_sem=recv_sem,
        device_id=(wa, gx), device_id_type=pl.DeviceIdType.MESH,
    )


def solve_kernel(chunks, planes, per_plane, gx_size, rhs_ref, local_ref, step_ref, full_ref, out_ref,
                 held, solved, near_out, near_in, far_out, far_in,
                 send_sem, recv_sem, own_sem, near_send, near_recv, far_send, far_recv,
                 back_send, back_recv, back_own):
    wa, gx = lax.axis_index("wa"), lax.axis_index("gx")
    lanes = near_out.shape[-1]
    rows = out_ref.shape[1]
    parts = held.shape[0]
    width = near_out.shape[1]
    per_part = chunks // parts
    z, x = wa // per_plane, wa % per_plane
    count = per_plane * gx_size
    me = x * gx_size + gx
    base = z * per_plane
    low = (z < planes // 2).astype(jnp.int32)
    inner = wa + per_plane * (2 * low - 1)
    outer = wa - per_plane * (2 * low - 1)
    middle = jnp.logical_and(z > 0, z < planes - 1)
    edge = jnp.logical_or(z == 0, z == planes - 1)
    barrier = pltpu.get_barrier_semaphore()

    def greet(to_wa, to_gx):
        pl.semaphore_signal(barrier, inc=1, device_id=(to_wa, to_gx),
                            device_id_type=pl.DeviceIdType.MESH)

    for k in range(1, count):
        peer = (me + k) % count
        greet(base + peer // gx_size, peer % gx_size)
    greet(inner, gx)

    @pl.when(middle)
    def _():
        greet(outer, gx)

    pl.semaphore_wait(barrier, count + middle.astype(jnp.int32))

    def place(c):
        return c // per_part, pl.ds(pl.multiple_of(c % per_part * lanes, LANES), lanes)

    def piece(c, k, to):
        part, cols = place(c)
        peer = (me + k) % count if to else (me + count - k) % count
        slot = me if to else peer
        peer_x, peer_gx = peer // gx_size, peer % gx_size
        return remote(rhs_ref.at[peer_x, part, peer_gx, :, cols], held.at[part, slot, :, cols],
                      send_sem.at[c, k], recv_sem.at[c, k], base + peer_x, peer_gx)

    def own_piece(c):
        part, cols = place(c)
        return pltpu.make_async_copy(rhs_ref.at[x, part, gx, :, cols], held.at[part, me, :, cols],
                                     own_sem.at[c])

    def near_from_edge(c, to):
        return remote(near_out.at[c], near_in.at[c], near_send.at[c], near_recv.at[c], to, gx)

    def near_from_middle(c):
        return remote(near_out.at[c], far_in.at[c], near_send.at[c], far_recv.at[c], inner, gx)

    def far_to_edge(c, to):
        return remote(far_out.at[c], far_in.at[c], far_send.at[c], far_recv.at[c], to, gx)

    def back(c, k, to):
        part, cols = place(c)
        peer = (x + k) % per_plane if to else (x + per_plane - k) % per_plane
        slot = x if to else peer
        return remote(solved.at[part, peer, :, cols], out_ref.at[slot * parts + part, :, cols],
                      back_send.at[c, k], back_recv.at[c, k], base + peer, gx)

    def back_own_piece(c):
        part, cols = place(c)
        return pltpu.make_async_copy(solved.at[part, x, :, cols],
                                     out_ref.at[x * parts + part, :, cols], back_own.at[c])

    def gathered(c):
        part, cols = place(c)
        return held[part, :, :, cols].reshape(per_plane * rows, lanes)

    def start_pieces(c, carry):
        own_piece(c).start()
        for k in range(1, count):
            piece(c, k, True).start()
        return carry

    def local_step(c):
        own_piece(c).wait()
        for k in range(1, count):
            piece(c, k, False).wait_recv()
        both = split_matmul(local_ref[...], gathered(c))
        near_out[c] = both[:width]
        far_out[c] = both[width:]

        @pl.when(edge)
        def _():
            near_in[c] = jnp.zeros((width, lanes), jnp.float32)
            near_from_edge(c, inner).start()

    def near_step(c):
        @pl.when(middle)
        def _():
            near_from_edge(c, outer).wait_recv()
            near_out[c] = near_out[c] + split_matmul(step_ref[0], near_in[c])
            near_from_middle(c).start()

    def far_step(c):
        @pl.when(middle)
        def _():
            near_from_middle(c).wait_recv()
            far_out[c] = far_out[c] + split_matmul(step_ref[1], far_in[c])
            far_to_edge(c, outer).start()

    def finish(c):
        @pl.when(edge)
        def _():
            far_to_edge(c, inner).wait_recv()

        part, cols = place(c)
        vectors = jnp.concatenate([gathered(c), near_in[c], far_in[c]], axis=0)
        result = split_matmul(full_ref[...], vectors)
        solved[part, :, :, cols] = result.reshape(per_plane, rows, lanes)
        back_own_piece(c).start()
        for k in range(1, per_plane):
            back(c, k, True).start()

    def drain(c, carry):
        for k in range(1, count):
            piece(c, k, True).wait_send()

        @pl.when(edge)
        def _():
            near_from_edge(c, inner).wait_send()

        @pl.when(middle)
        def _():
            near_from_middle(c).wait_send()
            far_to_edge(c, outer).wait_send()

        back_own_piece(c).wait()
        for k in range(1, per_plane):
            back(c, k, True).wait_send()
            back(c, k, False).wait_recv()
        return carry

    lags = ((local_step, 0), (near_step, 2), (far_step, 4), (finish, 6))

    def turn(t, carry):
        for step, lag in lags:
            c = t - lag

            @pl.when(jnp.logical_and(c >= 0, c < chunks))
            def _(step=step, c=c):
                step(c)

        return carry

    lax.fori_loop(0, chunks, start_pieces, 0)
    lax.fori_loop(0, chunks + lags[-1][1], turn, 0)
    lax.fori_loop(0, chunks, drain, 0)


def split_matmul(left, right):
    l_hi, r_hi = left.astype(jnp.bfloat16), right.astype(jnp.bfloat16)
    l_lo = (left - l_hi.astype(jnp.float32)).astype(jnp.bfloat16)
    r_lo = (right - r_hi.astype(jnp.float32)).astype(jnp.bfloat16)
    dot = functools.partial(jnp.dot, preferred_element_type=jnp.float32)
    return dot(l_hi, r_hi) + (dot(l_lo, r_hi) + dot(l_hi, r_lo))


def solve_across(wa, gx, rhs, block_inv, lower_mult):
    share, modes = rhs.shape[-2:]
    planes, per_plane, parts = 4, 2, 2
    rows = share * gx
    plane = per_plane * rows
    count = per_plane * gx
    nblocks, width = block_inv.shape[:2]
    reduce_op, back_op, dense = solve_matrices(block_inv, lower_mult)
    z = lax.axis_index("wa") // per_plane
    first, after = z * plane, (z + 1) * plane
    below = jnp.maximum(first - 1, 0) // width * width
    start = first // width * width
    end = (after - 1) // width * width
    above = jnp.minimum(after, nblocks * width - 1) // width * width

    def cut(table, row, height, column, span):
        return lax.dynamic_slice(table, (row, column), (height, span))

    up_local = cut(reduce_op, end, width, first, plane)
    up_step = cut(reduce_op, end, width, below, width)
    up_full = cut(dense, first, plane, below, width)
    down_local = cut(dense, start, width, first, plane)
    down_step = cut(back_op, start, width, above, width)
    down_full = cut(back_op, first, plane, above, width)
    low = z < planes // 2

    def ordered(up, down, axis):
        return jnp.where(low, jnp.concatenate([up, down], axis), jnp.concatenate([down, up], axis))

    local = ordered(up_local, down_local, 0)
    steps = ordered(up_step[None], down_step[None], 0)
    full = jnp.concatenate([cut(dense, first, plane, first, plane),
                            ordered(up_full, down_full, 1)], axis=1)
    lanes = 6 * LANES
    chunks = parts * modes // lanes
    dma = pltpu.SemaphoreType.DMA
    vmem = pl.BlockSpec(memory_space=pltpu.VMEM)
    anywhere = pl.BlockSpec(memory_space=pl.ANY)
    message = pltpu.VMEM((chunks, width, lanes), jnp.float32)
    return pl.pallas_call(
        functools.partial(solve_kernel, chunks, planes, per_plane, gx),
        out_shape=jax.ShapeDtypeStruct((per_plane * parts, rows, modes), jnp.float32),
        in_specs=[anywhere, vmem, vmem, vmem],
        out_specs=anywhere,
        scratch_shapes=[
            pltpu.VMEM((parts, count, share, modes), jnp.float32),
            pltpu.VMEM((parts, per_plane, rows, modes), jnp.float32),
            message, message, message, message,
            dma((chunks, count)),
            dma((chunks, count)),
            dma((chunks,)),
            dma((chunks,)),
            dma((chunks,)),
            dma((chunks,)),
            dma((chunks,)),
            dma((chunks, per_plane)),
            dma((chunks, per_plane)),
            dma((chunks,)),
        ],
        compiler_params=pltpu.CompilerParams(
            vmem_limit_bytes=44 * 1024 * 1024, collective_id=0, has_side_effects=True
        ),
    )(rhs, local, steps, full)


def body(wa, gx, field_a, field_b, keep_mask, block_inv, lower_mult):
    _, _, rows, modes = field_a.shape
    keep = keep_mask.astype(jnp.float32).reshape(1, modes)
    padded = -(-rows // (gx * ROWS)) * gx * ROWS
    share = padded // gx

    def spread(field):
        field = field.reshape(2, rows, modes)
        if padded != rows:
            field = jnp.pad(field, ((0, 0), (0, padded - rows), (0, 0)))
        field = field.reshape(2, gx, share, modes)
        return lax.all_to_all(field, "gx", split_axis=1, concat_axis=1, tiled=True)

    rhs = front(spread(field_a), spread(field_b), keep)
    if wa == 8 and gx == KXT and rows == padded and 2 * rows >= block_inv.shape[1]:
        solved = solve_across(wa, gx, rhs, block_inv, lower_mult)
        solved = solved.reshape(2, 2, 1, rows, modes)
        return (solved[0], solved[1])
    chunks = wa // 4
    width = modes // chunks
    rhs = jnp.moveaxis(rhs.reshape(2, 2, KXT, share, chunks, width), 4, 2)
    rhs = rhs.reshape(wa * gx, share, width)
    rhs = lax.all_to_all(rhs, ("wa", "gx"), split_axis=0, concat_axis=0, tiled=True)
    rhs = rhs.reshape(wa, padded, width)[:, :rows].reshape(wa * rows, width)
    solved = jnp.matmul(
        solve_matrices(block_inv, lower_mult)[2], rhs, precision=lax.Precision.HIGH
    ).reshape(wa, rows, width)
    solved = lax.all_to_all(solved, "wa", split_axis=0, concat_axis=0, tiled=True)
    solved = solved.reshape(2, 2, chunks, rows, width)
    solved = jnp.moveaxis(solved, 2, 3).reshape(2, 2, 1, rows, modes)
    return (solved[0], solved[1])


def solution(mesh):
    return jax.shard_map(
        functools.partial(body, mesh.shape["wa"], mesh.shape["gx"]),
        mesh=mesh,
        in_specs=(P(None, "gx", "wa", None), P(None, "gx", "wa", None), P(), P(), P()),
        out_specs=(P(None, "gx", "wa", None), P(None, "gx", "wa", None)),
        check_vma=False,
    )
```

```python
import functools
import math

import jax
import jax.numpy as jnp
import ml_dtypes
import numpy as np
from jax import lax
from jax.experimental import pallas as pl
from jax.experimental.pallas import tpu as pltpu
from jax.sharding import PartitionSpec as P

NL_COEFF = 0.25
LANES = 128
ROWS = 8
KXT = 4


def add(x, y):
    return (x[0] + y[0], x[1] + y[1])


def sub(x, y):
    return (x[0] - y[0], x[1] - y[1])


def scaled(x, factor):
    return (x[0] * factor, x[1] * factor)


def times_i(x, sign):
    return (-x[1], x[0]) if sign > 0 else (x[1], -x[0])


def times(x, re, im):
    return (x[0] * re - x[1] * im, x[0] * im + x[1] * re)


def dft3(x, sign):
    both, diff = add(x[1], x[2]), sub(x[1], x[2])
    mid = sub(x[0], scaled(both, 0.5))
    turn = times_i(scaled(diff, math.sqrt(0.75)), sign)
    return [add(x[0], both), add(mid, turn), sub(mid, turn)]


def dft4(x, sign):
    even, odd = add(x[0], x[2]), add(x[1], x[3])
    even_d, odd_d = sub(x[0], x[2]), times_i(sub(x[1], x[3]), sign)
    return [add(even, odd), add(even_d, odd_d), sub(even, odd), sub(even_d, odd_d)]


def dft5(x, sign):
    c1, c2 = math.cos(2 * math.pi / 5), math.cos(4 * math.pi / 5)
    s1, s2 = math.sin(2 * math.pi / 5), math.sin(4 * math.pi / 5)
    t1, t2 = add(x[1], x[4]), add(x[2], x[3])
    t3, t4 = sub(x[1], x[4]), sub(x[2], x[3])
    m1 = add(x[0], add(scaled(t1, c1), scaled(t2, c2)))
    m2 = add(x[0], add(scaled(t1, c2), scaled(t2, c1)))
    n1 = times_i(add(scaled(t3, s1), scaled(t4, s2)), sign)
    n2 = times_i(sub(scaled(t3, s2), scaled(t4, s1)), sign)
    return [add(x[0], add(t1, t2)), add(m1, n1), add(m2, n2), sub(m2, n2), sub(m1, n1)]


def dft9(x, sign):
    inner = [dft3([x[j], x[3 + j], x[6 + j]], sign) for j in range(3)]
    out = [None] * 9
    for d1 in range(3):
        terms = []
        for j in range(3):
            angle = sign * 2 * math.pi * j * d1 / 9
            term = inner[j][d1]
            terms.append(times(term, math.cos(angle), math.sin(angle)) if j * d1 else term)
        for d2, value in enumerate(dft3(terms, sign)):
            out[d1 + 3 * d2] = value
    return out


def dft45(load, store, mid_ref, sign, shape):
    zero = jnp.zeros(shape, jnp.float32)
    for beta in range(9):
        ins = [load((9 * alpha + 5 * beta) % 45) for alpha in range(5)]
        ins = [(zero, zero) if v is None else v for v in ins]
        for c, value in enumerate(dft5(ins, sign)):
            mid_ref[c, beta, 0], mid_ref[c, beta, 1] = value
    for c in range(5):
        outs = dft9([(mid_ref[c, b, 0], mid_ref[c, b, 1]) for b in range(9)], sign)
        for d in range(9):
            spot = next(b for b in range(45) if b % 5 == c and b % 9 == d)
            store(spot, outs[d])


def split_dot(x, w_hi, w_lo):
    hi = x.astype(jnp.bfloat16)
    lo = (x - hi.astype(jnp.float32)).astype(jnp.bfloat16)
    dot = functools.partial(jnp.dot, preferred_element_type=jnp.float32)
    return dot(hi, w_hi) + (dot(lo, w_hi) + dot(hi, w_lo))


def front_kernel(slab_ref, keep_ref, twist_ref, winv_ref, wfwd_ref, earlier_ref, out_ref,
                 plane_ref, mid_ref, za_ref, zb_ref, hat_ref):
    half = 15
    tile = (ROWS, LANES)
    for f in range(2):
        for t in range(30):
            cols = pl.ds(t * LANES, LANES)
            ins = [(slab_ref[k, f, 0, :, cols], slab_ref[k, f, 1, :, cols]) for k in range(KXT)]
            for x, value in enumerate(dft4(ins, 1)):
                plane_ref[x, f, t, 0], plane_ref[x, f, t, 1] = value

    def one_plane(x, carry):
        for f, z_ref in enumerate((za_ref, zb_ref)):
            def load(m1):
                if half <= m1 < 30:
                    return None
                t = m1 if m1 < half else m1 - half
                return (plane_ref[x, f, t, 0], plane_ref[x, f, t, 1])

            def store(b, value):
                re, im = times(value, twist_ref[0, b : b + 1, :], twist_ref[1, b : b + 1, :])
                z_ref[b * ROWS : (b + 1) * ROWS, :LANES] = re
                z_ref[b * ROWS : (b + 1) * ROWS, LANES:] = im

            dft45(load, store, mid_ref, 1, tile)
        grid_a = split_dot(za_ref[...], winv_ref[0], winv_ref[1])
        grid_b = split_dot(zb_ref[...], winv_ref[0], winv_ref[1])
        a = (grid_a[:, :LANES], grid_a[:, LANES:])
        b = (grid_b[:, :LANES], grid_b[:, LANES:])
        p = times(a, b[0], b[1])
        total, diff = add(a, b), sub(a, b)
        q = times(total, diff[0], diff[1])
        for z_ref, value in ((za_ref, p), (zb_ref, q)):
            z_ref[...] = split_dot(jnp.concatenate(value, axis=1), wfwd_ref[0], wfwd_ref[1])
        for f, z_ref in enumerate((za_ref, zb_ref)):
            def load(b):
                rows = slice(b * ROWS, (b + 1) * ROWS)
                value = (z_ref[rows, :LANES], z_ref[rows, LANES:])
                return times(value, twist_ref[0, b : b + 1, :], -twist_ref[1, b : b + 1, :])

            def store(m1, value):
                if half <= m1 < 30:
                    return
                t = m1 if m1 < half else m1 - half
                hat_ref[x, f, t, 0], hat_ref[x, f, t, 1] = value

            dft45(load, store, mid_ref, -1, tile)
        return carry

    lax.fori_loop(0, KXT, one_plane, 0)
    for f in range(2):
        for t in range(30):
            cols = pl.ds(t * LANES, LANES)
            keep = keep_ref[:, cols]
            ins = [(hat_ref[x, f, t, 0], hat_ref[x, f, t, 1]) for x in range(KXT)]
            for k, value in enumerate(dft4(ins, -1)):
                for part in range(2):
                    out_ref[f, part, k, :, cols] = (
                        slab_ref[k, f, part, :, cols] + value[part] * keep
                    )


def front_tables(modes):
    length = 3 * modes // 2
    b, m2 = np.arange(length // LANES)[:, None], np.arange(LANES)[None, :]
    twist = 2 * np.pi * (b * m2 % length) / length
    lane = np.arange(LANES)
    w = 2 * np.pi * (lane[:, None] * lane[None, :] % LANES) / LANES
    c, s = np.cos(w), np.sin(w)
    inv = np.block([[c, s], [-s, c]]) / math.sqrt(modes)
    fwd = np.block([[c, -s], [s, c]]) * (NL_COEFF / KXT / math.sqrt(length))

    def halves(table):
        hi = table.astype(np.float32).astype(ml_dtypes.bfloat16)
        lo = (table - hi.astype(np.float64)).astype(np.float32).astype(ml_dtypes.bfloat16)
        return np.stack([hi, lo])

    return np.stack([np.cos(twist), np.sin(twist)]).astype(np.float32), halves(inv), halves(fwd)


def front(slab, keep, all_rows, first_row, earlier):
    kxt, _, _, rows, modes = slab.shape
    first = first_row // ROWS
    assert kxt == KXT and modes == 30 * LANES and rows % ROWS == 0
    twist, inv, fwd = front_tables(modes)
    points = 45
    block = (2, 2, KXT, ROWS, modes)
    slab_block = (KXT, 2, 2, ROWS, modes)
    result = jax.ShapeDtypeStruct((2, 2, KXT, all_rows, modes), jnp.float32)
    if earlier is None:
        earlier = jnp.zeros((ROWS, LANES), jnp.float32)
        aliases = {}
    else:
        aliases = {5: 0}
    return pl.pallas_call(
        front_kernel,
        grid=(rows // ROWS,),
        out_shape=result,
        input_output_aliases=aliases,
        in_specs=[
            pl.BlockSpec(slab_block, lambda i: (0, 0, 0, i, 0)),
            pl.BlockSpec((1, modes), lambda i: (0, 0)),
            pl.BlockSpec(twist.shape, lambda i: (0, 0, 0)),
            pl.BlockSpec(inv.shape, lambda i: (0, 0, 0)),
            pl.BlockSpec(fwd.shape, lambda i: (0, 0, 0)),
            pl.BlockSpec(memory_space=pl.ANY),
        ],
        out_specs=pl.BlockSpec(block, lambda i: (0, 0, 0, i + first, 0)),
        scratch_shapes=[
            pltpu.VMEM((KXT, 2, 30, 2, ROWS, LANES), jnp.float32),
            pltpu.VMEM((5, 9, 2, ROWS, LANES), jnp.float32),
            pltpu.VMEM((points * ROWS, 2 * LANES), jnp.float32),
            pltpu.VMEM((points * ROWS, 2 * LANES), jnp.float32),
            pltpu.VMEM((KXT, 2, 30, 2, ROWS, LANES), jnp.float32),
        ],
        compiler_params=pltpu.CompilerParams(vmem_limit_bytes=40 * 1024 * 1024),
        cost_estimate=pl.CostEstimate(
            flops=rows * 32 * 5760 * 256 * 6, bytes_accessed=rows * 2**18, transcendentals=0
        ),
    )(slab, keep, jnp.asarray(twist), jnp.asarray(inv), jnp.asarray(fwd), earlier)


def solve_matrices(block_inv, lower_mult):
    count, width = block_inv.shape[:2]
    dot = functools.partial(jnp.matmul, precision=lax.Precision.HIGHEST)
    eye = jnp.eye(count * width, dtype=jnp.float32).reshape(count, width, count * width)
    reduced = [eye[0]]
    for j in range(1, count):
        reduced.append(eye[j] - dot(lower_mult[j - 1], reduced[-1]))
    back = [eye[-1]]
    for j in range(count - 2, -1, -1):
        back.insert(0, eye[j] - dot(lower_mult[j].T, back[0]))
    reduced = jnp.stack(reduced)
    back = jnp.concatenate(back, axis=0)
    dense = dot(back, dot(block_inv, reduced).reshape(count * width, count * width))
    return reduced.reshape(count * width, count * width), back, dense


def remote(src, dst, send_sem, recv_sem, wa, gx):
    return pltpu.make_async_remote_copy(
        src_ref=src, dst_ref=dst, send_sem=send_sem, recv_sem=recv_sem,
        device_id=(wa, gx), device_id_type=pl.DeviceIdType.MESH,
    )


def solve_kernel(chunks, planes, per_plane, gx_size, rhs_ref, local_ref, step_ref, full_ref, out_ref,
                 held, solved, near_out, near_in, far_out, far_in,
                 send_sem, recv_sem, own_sem, near_send, near_recv, far_send, far_recv,
                 back_send, back_recv, back_own):
    wa, gx = lax.axis_index("wa"), lax.axis_index("gx")
    lanes = near_out.shape[-1]
    rows = out_ref.shape[1]
    parts = held.shape[0]
    width = near_out.shape[1]
    per_part = chunks // parts
    z, x = wa // per_plane, wa % per_plane
    count = per_plane * gx_size
    me = x * gx_size + gx
    base = z * per_plane
    low = (z < planes // 2).astype(jnp.int32)
    inner = wa + per_plane * (2 * low - 1)
    outer = wa - per_plane * (2 * low - 1)
    middle = jnp.logical_and(z > 0, z < planes - 1)
    edge = jnp.logical_or(z == 0, z == planes - 1)
    barrier = pltpu.get_barrier_semaphore()

    def greet(to_wa, to_gx):
        pl.semaphore_signal(barrier, inc=1, device_id=(to_wa, to_gx),
                            device_id_type=pl.DeviceIdType.MESH)

    for k in range(1, count):
        peer = (me + k) % count
        greet(base + peer // gx_size, peer % gx_size)
    greet(inner, gx)

    @pl.when(middle)
    def _():
        greet(outer, gx)

    pl.semaphore_wait(barrier, count + middle.astype(jnp.int32))

    def place(c):
        return c // per_part, pl.ds(pl.multiple_of(c % per_part * lanes, LANES), lanes)

    def piece(c, k, to):
        part, cols = place(c)
        peer = (me + k) % count if to else (me + count - k) % count
        slot = me if to else peer
        peer_x, peer_gx = peer // gx_size, peer % gx_size
        return remote(rhs_ref.at[peer_x, part, peer_gx, :, cols], held.at[part, slot, :, cols],
                      send_sem.at[c, k], recv_sem.at[c, k], base + peer_x, peer_gx)

    def own_piece(c):
        part, cols = place(c)
        return pltpu.make_async_copy(rhs_ref.at[x, part, gx, :, cols], held.at[part, me, :, cols],
                                     own_sem.at[c])

    def near_from_edge(c, to):
        return remote(near_out.at[c], near_in.at[c], near_send.at[c], near_recv.at[c], to, gx)

    def near_from_middle(c):
        return remote(near_out.at[c], far_in.at[c], near_send.at[c], far_recv.at[c], inner, gx)

    def far_to_edge(c, to):
        return remote(far_out.at[c], far_in.at[c], far_send.at[c], far_recv.at[c], to, gx)

    def back(c, k, to):
        part, cols = place(c)
        peer = (x + k) % per_plane if to else (x + per_plane - k) % per_plane
        slot = x if to else peer
        return remote(solved.at[part, peer, :, cols], out_ref.at[slot * parts + part, :, cols],
                      back_send.at[c, k], back_recv.at[c, k], base + peer, gx)

    def back_own_piece(c):
        part, cols = place(c)
        return pltpu.make_async_copy(solved.at[part, x, :, cols],
                                     out_ref.at[x * parts + part, :, cols], back_own.at[c])

    def gathered(c):
        part, cols = place(c)
        return held[part, :, :, cols].reshape(per_plane * rows, lanes)

    def start_pieces(c, carry):
        own_piece(c).start()
        for k in range(1, count):
            piece(c, k, True).start()
        return carry

    def local_step(c):
        own_piece(c).wait()
        for k in range(1, count):
            piece(c, k, False).wait_recv()
        both = split_matmul(local_ref[...], gathered(c))
        near_out[c] = both[:width]
        far_out[c] = both[width:]

        @pl.when(edge)
        def _():
            near_in[c] = jnp.zeros((width, lanes), jnp.float32)
            near_from_edge(c, inner).start()

    def near_step(c):
        @pl.when(middle)
        def _():
            near_from_edge(c, outer).wait_recv()
            near_out[c] = near_out[c] + split_matmul(step_ref[0], near_in[c])
            near_from_middle(c).start()

    def far_step(c):
        @pl.when(middle)
        def _():
            near_from_middle(c).wait_recv()
            far_out[c] = far_out[c] + split_matmul(step_ref[1], far_in[c])
            far_to_edge(c, outer).start()

    def finish(c):
        @pl.when(edge)
        def _():
            far_to_edge(c, inner).wait_recv()

        part, cols = place(c)
        vectors = jnp.concatenate([gathered(c), near_in[c], far_in[c]], axis=0)
        result = split_matmul(full_ref[...], vectors)
        solved[part, :, :, cols] = result.reshape(per_plane, rows, lanes)
        back_own_piece(c).start()
        for k in range(1, per_plane):
            back(c, k, True).start()

    def drain(c, carry):
        for k in range(1, count):
            piece(c, k, True).wait_send()

        @pl.when(edge)
        def _():
            near_from_edge(c, inner).wait_send()

        @pl.when(middle)
        def _():
            near_from_middle(c).wait_send()
            far_to_edge(c, outer).wait_send()

        back_own_piece(c).wait()
        for k in range(1, per_plane):
            back(c, k, True).wait_send()
            back(c, k, False).wait_recv()
        return carry

    lags = ((local_step, 0), (near_step, 2), (far_step, 4), (finish, 6))

    def turn(t, carry):
        for step, lag in lags:
            c = t - lag

            @pl.when(jnp.logical_and(c >= 0, c < chunks))
            def _(step=step, c=c):
                step(c)

        return carry

    lax.fori_loop(0, chunks, start_pieces, 0)
    lax.fori_loop(0, chunks + lags[-1][1], turn, 0)
    lax.fori_loop(0, chunks, drain, 0)


def split_matmul(left, right):
    l_hi, r_hi = left.astype(jnp.bfloat16), right.astype(jnp.bfloat16)
    l_lo = (left - l_hi.astype(jnp.float32)).astype(jnp.bfloat16)
    r_lo = (right - r_hi.astype(jnp.float32)).astype(jnp.bfloat16)
    dot = functools.partial(jnp.dot, preferred_element_type=jnp.float32)
    return dot(l_hi, r_hi) + (dot(l_lo, r_hi) + dot(l_hi, r_lo))


def solve_across(wa, gx, rhs, block_inv, lower_mult):
    share, modes = rhs.shape[-2:]
    planes, per_plane, parts = 4, 2, 2
    rows = share * gx
    plane = per_plane * rows
    count = per_plane * gx
    nblocks, width = block_inv.shape[:2]
    reduce_op, back_op, dense = solve_matrices(block_inv, lower_mult)
    z = lax.axis_index("wa") // per_plane
    first, after = z * plane, (z + 1) * plane
    below = jnp.maximum(first - 1, 0) // width * width
    start = first // width * width
    end = (after - 1) // width * width
    above = jnp.minimum(after, nblocks * width - 1) // width * width

    def cut(table, row, height, column, span):
        return lax.dynamic_slice(table, (row, column), (height, span))

    up_local = cut(reduce_op, end, width, first, plane)
    up_step = cut(reduce_op, end, width, below, width)
    up_full = cut(dense, first, plane, below, width)
    down_local = cut(dense, start, width, first, plane)
    down_step = cut(back_op, start, width, above, width)
    down_full = cut(back_op, first, plane, above, width)
    low = z < planes // 2

    def ordered(up, down, axis):
        return jnp.where(low, jnp.concatenate([up, down], axis), jnp.concatenate([down, up], axis))

    local = ordered(up_local, down_local, 0)
    steps = ordered(up_step[None], down_step[None], 0)
    full = jnp.concatenate([cut(dense, first, plane, first, plane),
                            ordered(up_full, down_full, 1)], axis=1)
    lanes = 3 * LANES
    chunks = parts * modes // lanes
    dma = pltpu.SemaphoreType.DMA
    vmem = pl.BlockSpec(memory_space=pltpu.VMEM)
    anywhere = pl.BlockSpec(memory_space=pl.ANY)
    message = pltpu.VMEM((chunks, width, lanes), jnp.float32)
    return pl.pallas_call(
        functools.partial(solve_kernel, chunks, planes, per_plane, gx),
        out_shape=jax.ShapeDtypeStruct((per_plane * parts, rows, modes), jnp.float32),
        in_specs=[anywhere, vmem, vmem, vmem],
        out_specs=anywhere,
        scratch_shapes=[
            pltpu.VMEM((parts, count, share, modes), jnp.float32),
            pltpu.VMEM((parts, per_plane, rows, modes), jnp.float32),
            message, message, message, message,
            dma((chunks, count)),
            dma((chunks, count)),
            dma((chunks,)),
            dma((chunks,)),
            dma((chunks,)),
            dma((chunks,)),
            dma((chunks,)),
            dma((chunks, per_plane)),
            dma((chunks, per_plane)),
            dma((chunks,)),
        ],
        compiler_params=pltpu.CompilerParams(
            vmem_limit_bytes=44 * 1024 * 1024, collective_id=0, has_side_effects=True
        ),
    )(rhs, local, steps, full)


def body(wa, gx, field_a, field_b, keep_mask, block_inv, lower_mult):
    _, _, rows, modes = field_a.shape
    keep = keep_mask.astype(jnp.float32).reshape(1, modes)
    padded = -(-rows // (gx * ROWS)) * gx * ROWS
    share = padded // gx

    def spread(field):
        field = field.reshape(2, rows, modes)
        if padded != rows:
            field = jnp.pad(field, ((0, 0), (0, padded - rows), (0, 0)))
        return field.reshape(2, gx, share, modes)

    fields = (spread(field_a), spread(field_b))
    cut = share // ROWS * 2 // 3 * ROWS
    rhs, slab = None, None
    for first, last in ((0, cut), (cut, share)):
        if first < last:
            part = jnp.stack([field[:, :, first:last] for field in fields])
            part = jnp.moveaxis(part, 2, 0)
            if slab is not None:
                part, slab = lax.optimization_barrier((part, slab))
                rhs = front(slab, keep, share, 0, None)
            slab = lax.all_to_all(part, "gx", split_axis=0, concat_axis=0, tiled=True)
            begin = first
    rhs = front(slab, keep, share, begin, rhs)
    if wa == 8 and gx == KXT and rows == padded and 2 * rows >= block_inv.shape[1]:
        solved = solve_across(wa, gx, rhs, block_inv, lower_mult)
        solved = solved.reshape(2, 2, 1, rows, modes)
        return (solved[0], solved[1])
    chunks = wa // 4
    width = modes // chunks
    rhs = jnp.moveaxis(rhs.reshape(2, 2, KXT, share, chunks, width), 4, 2)
    rhs = rhs.reshape(wa * gx, share, width)
    rhs = lax.all_to_all(rhs, ("wa", "gx"), split_axis=0, concat_axis=0, tiled=True)
    rhs = rhs.reshape(wa, padded, width)[:, :rows].reshape(wa * rows, width)
    solved = jnp.matmul(
        solve_matrices(block_inv, lower_mult)[2], rhs, precision=lax.Precision.HIGH
    ).reshape(wa, rows, width)
    solved = lax.all_to_all(solved, "wa", split_axis=0, concat_axis=0, tiled=True)
    solved = solved.reshape(2, 2, chunks, rows, width)
    solved = jnp.moveaxis(solved, 2, 3).reshape(2, 2, 1, rows, modes)
    return (solved[0], solved[1])


def solution(mesh):
    return jax.shard_map(
        functools.partial(body, mesh.shape["wa"], mesh.shape["gx"]),
        mesh=mesh,
        in_specs=(P(None, "gx", "wa", None), P(None, "gx", "wa", None), P(), P(), P()),
        out_specs=(P(None, "gx", "wa", None), P(None, "gx", "wa", None)),
        check_vma=False,
    )
```

```python
import functools
import math

import jax
import jax.numpy as jnp
import ml_dtypes
import numpy as np
from jax import lax
from jax.experimental import pallas as pl
from jax.experimental.pallas import tpu as pltpu
from jax.sharding import PartitionSpec as P

NL_COEFF = 0.25
LANES = 128
ROWS = 8
KXT = 4


def add(x, y):
    return (x[0] + y[0], x[1] + y[1])


def sub(x, y):
    return (x[0] - y[0], x[1] - y[1])


def scaled(x, factor):
    return (x[0] * factor, x[1] * factor)


def times_i(x, sign):
    return (-x[1], x[0]) if sign > 0 else (x[1], -x[0])


def times(x, re, im):
    return (x[0] * re - x[1] * im, x[0] * im + x[1] * re)


def dft3(x, sign):
    both, diff = add(x[1], x[2]), sub(x[1], x[2])
    mid = sub(x[0], scaled(both, 0.5))
    turn = times_i(scaled(diff, math.sqrt(0.75)), sign)
    return [add(x[0], both), add(mid, turn), sub(mid, turn)]


def dft4(x, sign):
    even, odd = add(x[0], x[2]), add(x[1], x[3])
    even_d, odd_d = sub(x[0], x[2]), times_i(sub(x[1], x[3]), sign)
    return [add(even, odd), add(even_d, odd_d), sub(even, odd), sub(even_d, odd_d)]


def dft5(x, sign):
    c1, c2 = math.cos(2 * math.pi / 5), math.cos(4 * math.pi / 5)
    s1, s2 = math.sin(2 * math.pi / 5), math.sin(4 * math.pi / 5)
    t1, t2 = add(x[1], x[4]), add(x[2], x[3])
    t3, t4 = sub(x[1], x[4]), sub(x[2], x[3])
    m1 = add(x[0], add(scaled(t1, c1), scaled(t2, c2)))
    m2 = add(x[0], add(scaled(t1, c2), scaled(t2, c1)))
    n1 = times_i(add(scaled(t3, s1), scaled(t4, s2)), sign)
    n2 = times_i(sub(scaled(t3, s2), scaled(t4, s1)), sign)
    return [add(x[0], add(t1, t2)), add(m1, n1), add(m2, n2), sub(m2, n2), sub(m1, n1)]


def dft9(x, sign):
    inner = [dft3([x[j], x[3 + j], x[6 + j]], sign) for j in range(3)]
    out = [None] * 9
    for d1 in range(3):
        terms = []
        for j in range(3):
            angle = sign * 2 * math.pi * j * d1 / 9
            term = inner[j][d1]
            terms.append(times(term, math.cos(angle), math.sin(angle)) if j * d1 else term)
        for d2, value in enumerate(dft3(terms, sign)):
            out[d1 + 3 * d2] = value
    return out


def dft45(load, store, mid_ref, sign, shape):
    zero = jnp.zeros(shape, jnp.float32)
    for beta in range(9):
        ins = [load((9 * alpha + 5 * beta) % 45) for alpha in range(5)]
        ins = [(zero, zero) if v is None else v for v in ins]
        for c, value in enumerate(dft5(ins, sign)):
            mid_ref[c, beta, 0], mid_ref[c, beta, 1] = value
    for c in range(5):
        outs = dft9([(mid_ref[c, b, 0], mid_ref[c, b, 1]) for b in range(9)], sign)
        for d in range(9):
            spot = next(b for b in range(45) if b % 5 == c and b % 9 == d)
            store(spot, outs[d])


def split_dot(x, w_hi, w_lo):
    hi = x.astype(jnp.bfloat16)
    lo = (x - hi.astype(jnp.float32)).astype(jnp.bfloat16)
    dot = functools.partial(jnp.dot, preferred_element_type=jnp.float32)
    return dot(hi, w_hi) + (dot(lo, w_hi) + dot(hi, w_lo))


def front_kernel(slab_ref, keep_ref, twist_ref, winv_ref, wfwd_ref, earlier_ref, out_ref,
                 plane_ref, mid_ref, za_ref, zb_ref, hat_ref):
    half = 15
    tile = (ROWS, LANES)
    for f in range(2):
        for t in range(30):
            cols = pl.ds(t * LANES, LANES)
            ins = [(slab_ref[k, f, 0, :, cols], slab_ref[k, f, 1, :, cols]) for k in range(KXT)]
            for x, value in enumerate(dft4(ins, 1)):
                plane_ref[x, f, t, 0], plane_ref[x, f, t, 1] = value

    def one_plane(x, carry):
        for f, z_ref in enumerate((za_ref, zb_ref)):
            def load(m1):
                if half <= m1 < 30:
                    return None
                t = m1 if m1 < half else m1 - half
                return (plane_ref[x, f, t, 0], plane_ref[x, f, t, 1])

            def store(b, value):
                re, im = times(value, twist_ref[0, b : b + 1, :], twist_ref[1, b : b + 1, :])
                z_ref[b * ROWS : (b + 1) * ROWS, :LANES] = re
                z_ref[b * ROWS : (b + 1) * ROWS, LANES:] = im

            dft45(load, store, mid_ref, 1, tile)
        grid_a = split_dot(za_ref[...], winv_ref[0], winv_ref[1])
        grid_b = split_dot(zb_ref[...], winv_ref[0], winv_ref[1])
        a = (grid_a[:, :LANES], grid_a[:, LANES:])
        b = (grid_b[:, :LANES], grid_b[:, LANES:])
        p = times(a, b[0], b[1])
        total, diff = add(a, b), sub(a, b)
        q = times(total, diff[0], diff[1])
        for z_ref, value in ((za_ref, p), (zb_ref, q)):
            z_ref[...] = split_dot(jnp.concatenate(value, axis=1), wfwd_ref[0], wfwd_ref[1])
        for f, z_ref in enumerate((za_ref, zb_ref)):
            def load(b):
                rows = slice(b * ROWS, (b + 1) * ROWS)
                value = (z_ref[rows, :LANES], z_ref[rows, LANES:])
                return times(value, twist_ref[0, b : b + 1, :], -twist_ref[1, b : b + 1, :])

            def store(m1, value):
                if half <= m1 < 30:
                    return
                t = m1 if m1 < half else m1 - half
                hat_ref[x, f, t, 0], hat_ref[x, f, t, 1] = value

            dft45(load, store, mid_ref, -1, tile)
        return carry

    lax.fori_loop(0, KXT, one_plane, 0)
    for f in range(2):
        for t in range(30):
            cols = pl.ds(t * LANES, LANES)
            keep = keep_ref[:, cols]
            ins = [(hat_ref[x, f, t, 0], hat_ref[x, f, t, 1]) for x in range(KXT)]
            for k, value in enumerate(dft4(ins, -1)):
                for part in range(2):
                    out_ref[f, part, k, :, cols] = (
                        slab_ref[k, f, part, :, cols] + value[part] * keep
                    )


def front_tables(modes):
    length = 3 * modes // 2
    b, m2 = np.arange(length // LANES)[:, None], np.arange(LANES)[None, :]
    twist = 2 * np.pi * (b * m2 % length) / length
    lane = np.arange(LANES)
    w = 2 * np.pi * (lane[:, None] * lane[None, :] % LANES) / LANES
    c, s = np.cos(w), np.sin(w)
    inv = np.block([[c, s], [-s, c]]) / math.sqrt(modes)
    fwd = np.block([[c, -s], [s, c]]) * (NL_COEFF / KXT / math.sqrt(length))

    def halves(table):
        hi = table.astype(np.float32).astype(ml_dtypes.bfloat16)
        lo = (table - hi.astype(np.float64)).astype(np.float32).astype(ml_dtypes.bfloat16)
        return np.stack([hi, lo])

    return np.stack([np.cos(twist), np.sin(twist)]).astype(np.float32), halves(inv), halves(fwd)


def front(slab, keep, all_rows, first_row, earlier):
    kxt, _, _, rows, modes = slab.shape
    first = first_row // ROWS
    assert kxt == KXT and modes == 30 * LANES and rows % ROWS == 0
    twist, inv, fwd = front_tables(modes)
    points = 45
    block = (2, 2, KXT, ROWS, modes)
    slab_block = (KXT, 2, 2, ROWS, modes)
    result = jax.ShapeDtypeStruct((2, 2, KXT, all_rows, modes), jnp.float32)
    if earlier is None:
        earlier = jnp.zeros((ROWS, LANES), jnp.float32)
        aliases = {}
    else:
        aliases = {5: 0}
    return pl.pallas_call(
        front_kernel,
        grid=(rows // ROWS,),
        out_shape=result,
        input_output_aliases=aliases,
        in_specs=[
            pl.BlockSpec(slab_block, lambda i: (0, 0, 0, i, 0)),
            pl.BlockSpec((1, modes), lambda i: (0, 0)),
            pl.BlockSpec(twist.shape, lambda i: (0, 0, 0)),
            pl.BlockSpec(inv.shape, lambda i: (0, 0, 0)),
            pl.BlockSpec(fwd.shape, lambda i: (0, 0, 0)),
            pl.BlockSpec(memory_space=pl.ANY),
        ],
        out_specs=pl.BlockSpec(block, lambda i: (0, 0, 0, i + first, 0)),
        scratch_shapes=[
            pltpu.VMEM((KXT, 2, 30, 2, ROWS, LANES), jnp.float32),
            pltpu.VMEM((5, 9, 2, ROWS, LANES), jnp.float32),
            pltpu.VMEM((points * ROWS, 2 * LANES), jnp.float32),
            pltpu.VMEM((points * ROWS, 2 * LANES), jnp.float32),
            pltpu.VMEM((KXT, 2, 30, 2, ROWS, LANES), jnp.float32),
        ],
        compiler_params=pltpu.CompilerParams(vmem_limit_bytes=40 * 1024 * 1024),
        cost_estimate=pl.CostEstimate(
            flops=rows * 32 * 5760 * 256 * 6, bytes_accessed=rows * 2**18, transcendentals=0
        ),
    )(slab, keep, jnp.asarray(twist), jnp.asarray(inv), jnp.asarray(fwd), earlier)


def solve_matrices(block_inv, lower_mult):
    count, width = block_inv.shape[:2]
    dot = functools.partial(jnp.matmul, precision=lax.Precision.HIGHEST)
    eye = jnp.eye(count * width, dtype=jnp.float32).reshape(count, width, count * width)
    reduced = [eye[0]]
    for j in range(1, count):
        reduced.append(eye[j] - dot(lower_mult[j - 1], reduced[-1]))
    back = [eye[-1]]
    for j in range(count - 2, -1, -1):
        back.insert(0, eye[j] - dot(lower_mult[j].T, back[0]))
    reduced = jnp.stack(reduced)
    back = jnp.concatenate(back, axis=0)
    dense = dot(back, dot(block_inv, reduced).reshape(count * width, count * width))
    return reduced.reshape(count * width, count * width), back, dense


def remote(src, dst, send_sem, recv_sem, wa, gx):
    return pltpu.make_async_remote_copy(
        src_ref=src, dst_ref=dst, send_sem=send_sem, recv_sem=recv_sem,
        device_id=(wa, gx), device_id_type=pl.DeviceIdType.MESH,
    )


def solve_kernel(chunks, planes, per_plane, gx_size, rhs_ref, local_ref, step_ref, full_ref, out_ref,
                 held, solved, near_out, near_in, far_out, far_in,
                 send_sem, recv_sem, own_sem, near_send, near_recv, far_send, far_recv,
                 back_send, back_recv, back_own):
    wa, gx = lax.axis_index("wa"), lax.axis_index("gx")
    lanes = near_out.shape[-1]
    rows = out_ref.shape[1]
    parts = held.shape[0]
    width = near_out.shape[1]
    per_part = chunks // parts
    z, x = wa // per_plane, wa % per_plane
    count = per_plane * gx_size
    me = x * gx_size + gx
    base = z * per_plane
    low = (z < planes // 2).astype(jnp.int32)
    inner = wa + per_plane * (2 * low - 1)
    outer = wa - per_plane * (2 * low - 1)
    middle = jnp.logical_and(z > 0, z < planes - 1)
    edge = jnp.logical_or(z == 0, z == planes - 1)
    barrier = pltpu.get_barrier_semaphore()

    def greet(to_wa, to_gx):
        pl.semaphore_signal(barrier, inc=1, device_id=(to_wa, to_gx),
                            device_id_type=pl.DeviceIdType.MESH)

    for k in range(1, count):
        peer = (me + k) % count
        greet(base + peer // gx_size, peer % gx_size)
    greet(inner, gx)

    @pl.when(middle)
    def _():
        greet(outer, gx)

    pl.semaphore_wait(barrier, count + middle.astype(jnp.int32))

    def place(c):
        return c // per_part, pl.ds(pl.multiple_of(c % per_part * lanes, LANES), lanes)

    def piece(c, k, to):
        part, cols = place(c)
        peer = (me + k) % count if to else (me + count - k) % count
        slot = me if to else peer
        peer_x, peer_gx = peer // gx_size, peer % gx_size
        return remote(rhs_ref.at[peer_x, part, peer_gx, :, cols], held.at[part, slot, :, cols],
                      send_sem.at[c, k], recv_sem.at[c, k], base + peer_x, peer_gx)

    def own_piece(c):
        part, cols = place(c)
        return pltpu.make_async_copy(rhs_ref.at[x, part, gx, :, cols], held.at[part, me, :, cols],
                                     own_sem.at[c])

    def near_from_edge(c, to):
        return remote(near_out.at[c], near_in.at[c], near_send.at[c], near_recv.at[c], to, gx)

    def near_from_middle(c):
        return remote(near_out.at[c], far_in.at[c], near_send.at[c], far_recv.at[c], inner, gx)

    def far_to_edge(c, to):
        return remote(far_out.at[c], far_in.at[c], far_send.at[c], far_recv.at[c], to, gx)

    def back(c, k, to):
        part, cols = place(c)
        peer = (x + k) % per_plane if to else (x + per_plane - k) % per_plane
        slot = x if to else peer
        return remote(solved.at[part, peer, :, cols], out_ref.at[slot * parts + part, :, cols],
                      back_send.at[c, k], back_recv.at[c, k], base + peer, gx)

    def back_own_piece(c):
        part, cols = place(c)
        return pltpu.make_async_copy(solved.at[part, x, :, cols],
                                     out_ref.at[x * parts + part, :, cols], back_own.at[c])

    def gathered(c):
        part, cols = place(c)
        return held[part, :, :, cols].reshape(per_plane * rows, lanes)

    def start_pieces(c, carry):
        own_piece(c).start()
        for k in range(1, count):
            piece(c, k, True).start()
        return carry

    def local_step(c):
        own_piece(c).wait()
        for k in range(1, count):
            piece(c, k, False).wait_recv()
        both = split_matmul(local_ref[...], gathered(c))
        near_out[c] = both[:width]
        far_out[c] = both[width:]

        @pl.when(edge)
        def _():
            near_in[c] = jnp.zeros((width, lanes), jnp.float32)
            near_from_edge(c, inner).start()

    def near_step(c):
        @pl.when(middle)
        def _():
            near_from_edge(c, outer).wait_recv()
            near_out[c] = near_out[c] + split_matmul(step_ref[0], near_in[c])
            near_from_middle(c).start()

    def far_step(c):
        @pl.when(middle)
        def _():
            near_from_middle(c).wait_recv()
            far_out[c] = far_out[c] + split_matmul(step_ref[1], far_in[c])
            far_to_edge(c, outer).start()

    def finish(c):
        @pl.when(edge)
        def _():
            far_to_edge(c, inner).wait_recv()

        part, cols = place(c)
        vectors = jnp.concatenate([gathered(c), near_in[c], far_in[c]], axis=0)
        result = split_matmul(full_ref[...], vectors)
        solved[part, :, :, cols] = result.reshape(per_plane, rows, lanes)
        back_own_piece(c).start()
        for k in range(1, per_plane):
            back(c, k, True).start()

    def drain(c, carry):
        for k in range(1, count):
            piece(c, k, True).wait_send()

        @pl.when(edge)
        def _():
            near_from_edge(c, inner).wait_send()

        @pl.when(middle)
        def _():
            near_from_middle(c).wait_send()
            far_to_edge(c, outer).wait_send()

        back_own_piece(c).wait()
        for k in range(1, per_plane):
            back(c, k, True).wait_send()
            back(c, k, False).wait_recv()
        return carry

    lags = ((local_step, 0), (near_step, 2), (far_step, 4), (finish, 6))

    def turn(t, carry):
        for step, lag in lags:
            c = t - lag

            @pl.when(jnp.logical_and(c >= 0, c < chunks))
            def _(step=step, c=c):
                step(c)

        return carry

    lax.fori_loop(0, chunks, start_pieces, 0)
    lax.fori_loop(0, chunks + lags[-1][1], turn, 0)
    lax.fori_loop(0, chunks, drain, 0)


def split_matmul(left, right):
    l_hi, r_hi = left.astype(jnp.bfloat16), right.astype(jnp.bfloat16)
    l_lo = (left - l_hi.astype(jnp.float32)).astype(jnp.bfloat16)
    r_lo = (right - r_hi.astype(jnp.float32)).astype(jnp.bfloat16)
    dot = functools.partial(jnp.dot, preferred_element_type=jnp.float32)
    return dot(l_hi, r_hi) + (dot(l_lo, r_hi) + dot(l_hi, r_lo))


def plane_matrices(rows, block_inv, lower_mult):
    planes, per_plane = 4, 2
    plane = per_plane * rows
    nblocks, width = block_inv.shape[:2]
    reduce_op, back_op, dense = solve_matrices(block_inv, lower_mult)
    z = lax.axis_index("wa") // per_plane
    first, after = z * plane, (z + 1) * plane
    below = jnp.maximum(first - 1, 0) // width * width
    start = first // width * width
    end = (after - 1) // width * width
    above = jnp.minimum(after, nblocks * width - 1) // width * width

    def cut(table, row, height, column, span):
        return lax.dynamic_slice(table, (row, column), (height, span))

    up_local = cut(reduce_op, end, width, first, plane)
    up_step = cut(reduce_op, end, width, below, width)
    up_full = cut(dense, first, plane, below, width)
    down_local = cut(dense, start, width, first, plane)
    down_step = cut(back_op, start, width, above, width)
    down_full = cut(back_op, first, plane, above, width)
    low = z < planes // 2

    def ordered(up, down, axis):
        return jnp.where(low, jnp.concatenate([up, down], axis), jnp.concatenate([down, up], axis))

    local = ordered(up_local, down_local, 0)
    steps = ordered(up_step[None], down_step[None], 0)
    full = jnp.concatenate([cut(dense, first, plane, first, plane),
                            ordered(up_full, down_full, 1)], axis=1)
    return local, steps, full


def solve_across(wa, gx, rhs, local, steps, full):
    share, modes = rhs.shape[-2:]
    planes, per_plane, parts = 4, 2, 2
    rows = share * gx
    count = per_plane * gx
    width = steps.shape[1]
    lanes = 3 * LANES
    chunks = parts * modes // lanes
    dma = pltpu.SemaphoreType.DMA
    vmem = pl.BlockSpec(memory_space=pltpu.VMEM)
    anywhere = pl.BlockSpec(memory_space=pl.ANY)
    message = pltpu.VMEM((chunks, width, lanes), jnp.float32)
    return pl.pallas_call(
        functools.partial(solve_kernel, chunks, planes, per_plane, gx),
        out_shape=jax.ShapeDtypeStruct((per_plane * parts, rows, modes), jnp.float32),
        in_specs=[anywhere, vmem, vmem, vmem],
        out_specs=anywhere,
        scratch_shapes=[
            pltpu.VMEM((parts, count, share, modes), jnp.float32),
            pltpu.VMEM((parts, per_plane, rows, modes), jnp.float32),
            message, message, message, message,
            dma((chunks, count)),
            dma((chunks, count)),
            dma((chunks,)),
            dma((chunks,)),
            dma((chunks,)),
            dma((chunks,)),
            dma((chunks,)),
            dma((chunks, per_plane)),
            dma((chunks, per_plane)),
            dma((chunks,)),
        ],
        compiler_params=pltpu.CompilerParams(
            vmem_limit_bytes=44 * 1024 * 1024, collective_id=0, has_side_effects=True
        ),
    )(rhs, local, steps, full)


def body(wa, gx, field_a, field_b, keep_mask, block_inv, lower_mult):
    _, _, rows, modes = field_a.shape
    keep = keep_mask.astype(jnp.float32).reshape(1, modes)
    padded = -(-rows // (gx * ROWS)) * gx * ROWS
    share = padded // gx

    def spread(field):
        field = field.reshape(2, rows, modes)
        if padded != rows:
            field = jnp.pad(field, ((0, 0), (0, padded - rows), (0, 0)))
        return field.reshape(2, gx, share, modes)

    fields = (spread(field_a), spread(field_b))
    cut = share // ROWS * 2 // 3 * ROWS
    chained = wa == 8 and gx == KXT and rows == padded and 2 * rows >= block_inv.shape[1]
    matrices = plane_matrices(rows, block_inv, lower_mult) if chained else ()
    rhs, slab = None, None
    for first, last in ((0, cut), (cut, share)):
        if first < last:
            part = jnp.stack([field[:, :, first:last] for field in fields])
            part = jnp.moveaxis(part, 2, 0)
            if slab is not None:
                part, slab, matrices = lax.optimization_barrier((part, slab, matrices))
                rhs = front(slab, keep, share, 0, None)
            slab = lax.all_to_all(part, "gx", split_axis=0, concat_axis=0, tiled=True)
            begin = first
    rhs = front(slab, keep, share, begin, rhs)
    if chained:
        solved = solve_across(wa, gx, rhs, *matrices)
        solved = solved.reshape(2, 2, 1, rows, modes)
        return (solved[0], solved[1])
    chunks = wa // 4
    width = modes // chunks
    rhs = jnp.moveaxis(rhs.reshape(2, 2, KXT, share, chunks, width), 4, 2)
    rhs = rhs.reshape(wa * gx, share, width)
    rhs = lax.all_to_all(rhs, ("wa", "gx"), split_axis=0, concat_axis=0, tiled=True)
    rhs = rhs.reshape(wa, padded, width)[:, :rows].reshape(wa * rows, width)
    solved = jnp.matmul(
        solve_matrices(block_inv, lower_mult)[2], rhs, precision=lax.Precision.HIGH
    ).reshape(wa, rows, width)
    solved = lax.all_to_all(solved, "wa", split_axis=0, concat_axis=0, tiled=True)
    solved = solved.reshape(2, 2, chunks, rows, width)
    solved = jnp.moveaxis(solved, 2, 3).reshape(2, 2, 1, rows, modes)
    return (solved[0], solved[1])


def solution(mesh):
    return jax.shard_map(
        functools.partial(body, mesh.shape["wa"], mesh.shape["gx"]),
        mesh=mesh,
        in_specs=(P(None, "gx", "wa", None), P(None, "gx", "wa", None), P(), P(), P()),
        out_specs=(P(None, "gx", "wa", None), P(None, "gx", "wa", None)),
        check_vma=False,
    )
```
